32 devices in a mesh: groups: 2 (over y), seq: 8 (over z, x), head: 1, sub: 2 (over core).
Axes of the slice: x: 2, y: 2, z: 4, core: 2. Of those that a mesh axis runs over, the one named last changes fastest.
Arguments:
- queries: bfloat16 [8, 32768, 512], P('head', ('groups', 'seq', 'sub')), parts along dimension 1, may hold values from -6 to 6
- keys: bfloat16 [8, 32768, 512], P('head', ('groups', 'seq', 'sub')), parts along dimension 1, may hold values from -6 to 6
- values: bfloat16 [8, 32768, 512], P('head', ('groups', 'seq', 'sub')), parts along dimension 1, may hold values from -6 to 6
- lr_codes: int32 [8, 32768], P('head', ('groups', 'seq', 'sub')), parts along dimension 1, may hold values from 0 to 15
- fast_gate: float32 [8, 512, 512], P('head', ('seq', 'sub')), may hold values from -0.25 to 0.25
- fast_up: float32 [8, 512, 512], P('head', ('seq', 'sub')), may hold values from -0.25 to 0.25
- fast_down: float32 [8, 512, 512], P('head', ('seq', 'sub')), may hold values from -0.25 to 0.25
Outputs:
- fast_out: bfloat16 [8, 32768, 512], P('head', ('groups', 'seq', 'sub')), parts along dimension 1
The draws below stay inside these ranges and needn't reach their ends.
There are 2 independent parts, one for each index of `groups`. The reference program is written for one: setup_inputs(seed, part) draws one part's arguments, and reference() takes and returns one part's arrays. A program takes and returns all parts, laid end to end along the dimension named above; an argument that names none is the same for every part. Nothing has to cross between parts.
All inputs are finite; a program needn't handle non-finite values.
Results may differ from the reference program's by a relative error of at most 0.0085.
Values may be sent and summed in bfloat16 or wider, within the bound.
A program may use at most 192 MiB of HBM per device.

```python
import jax
import jax.numpy as jnp
from jax import lax

HEADS = 8
FD = 512
FH = 512
BLOCK = 16384


def plant(entries, key, smallest, largest):
    longest = entries.shape.index(max(entries.shape))
    spots = []
    for shift in (0, 1):
        where = [jax.random.randint(jax.random.fold_in(key, axis), (), 0, length) for axis, length in enumerate(entries.shape)]
        where[longest] = (where[longest] + shift) % entries.shape[longest]
        spots.append(tuple(where))
    return entries.at[spots[0]].set(smallest).at[spots[1]].set(largest)


def raised(drawn, key, source, target, blocks, factor):
    owner, partner = [(jnp.arange(drawn.shape[dim]) // (drawn.shape[dim] // blocks)).reshape([-1 if axis == dim else 1 for axis in range(drawn.ndim)]) for dim in (source, target)]
    chosen = jax.random.permutation(key, blocks)[partner]
    strong = (owner == chosen) | (owner == (partner + blocks // 2) % blocks)
    return jnp.where(strong, factor * drawn, drawn)


def block_levels(stream_key, dims, cuts, smallest, top_value):
    def one(position, blocks):
        draws = jax.random.uniform(jax.random.fold_in(jax.random.fold_in(stream_key, 6), position), (blocks,), jnp.float32, smallest / len(cuts), top_value / len(cuts))
        return jnp.repeat(jnp.exp(draws), dims[position] // blocks).reshape((-1,) + (1,) * (len(dims) - position - 1))

    loudness = one(*cuts[0])
    for cut in cuts[1:]:
        loudness = loudness * one(*cut)
    return loudness


def scatter_about(stream_key, extent, scale, limit, pieces=(), kind=jnp.bfloat16):
    result = scale * jax.random.normal(stream_key, extent, jnp.float32)
    if pieces:
        result = result * block_levels(stream_key, extent, pieces, -0.22, 0.18)
    return jnp.clip(result, -limit, limit).astype(kind)


def bell_draw_with(rng, shape, width, limit, pieces, heavy, held_as=jnp.bfloat16):
    array = width * jax.random.normal(rng, shape, jnp.float32)
    if pieces:
        array = array * block_levels(rng, shape, pieces, -0.22, 0.18)
    return jnp.clip(raised(array, jax.random.fold_in(rng, 3), *heavy), -limit, limit).astype(held_as)


def setup_inputs(seed: int = 0, part: int = 0) -> dict:
    arg_keys = jax.random.split(jax.random.key(seed), 8)
    part_keys = jax.random.split(jax.random.fold_in(arg_keys[7], part), 8)
    return {
        "queries": scatter_about(part_keys[0], (HEADS, BLOCK, FD), 1.0, 6.0, ((1, 16),)),
        "keys": bell_draw_with(part_keys[1], (HEADS, BLOCK, FD), 1.0, 6.0, ((1, 16),), (1, 2, 16, 2.0)),
        "values": scatter_about(part_keys[2], (HEADS, BLOCK, FD), 1.0, 6.0, ((1, 16),)),
        "lr_codes": plant(jax.random.randint(part_keys[3], (HEADS, BLOCK), 0, 16), jax.random.fold_in(part_keys[3], 1), 0, 15).astype(jnp.int32),
        "fast_gate": scatter_about(arg_keys[4], (HEADS, FD, FH), FD ** -0.5, 0.25, ((1, 16),), jnp.float32),
        "fast_up": scatter_about(arg_keys[5], (HEADS, FD, FH), FD ** -0.5, 0.25, ((1, 16),), jnp.float32),
        "fast_down": scatter_about(arg_keys[6], (HEADS, FH, FD), FH ** -0.5, 0.25, ((1, 16),), jnp.float32),
    }


EPSILON = 1e-06
STEP_SIZE = 0.5

def renew(weight, grad):
    scale = STEP_SIZE * jnp.sqrt(jnp.sum(weight * weight) + EPSILON) / jnp.sqrt(jnp.sum(grad * grad) + EPSILON)
    moved = weight - scale * grad
    ratio = jnp.sqrt((lax.optimization_barrier(jnp.sum(weight * weight, axis=0)) + EPSILON) / (lax.optimization_barrier(jnp.sum(moved * moved, axis=0)) + EPSILON))
    return moved * ratio[None, :]

def one_head(operands):
    queries, keys, values, codes, gate_w, up_w, down_w = operands
    gate_b = gate_w.astype(jnp.bfloat16)
    up_b = up_w.astype(jnp.bfloat16)
    down_b = down_w.astype(jnp.bfloat16)
    gate_pre = jnp.dot(keys, gate_b, preferred_element_type=jnp.float32)
    up_pre = jnp.dot(keys, up_b, preferred_element_type=jnp.float32)
    sigmoid_gate = jax.nn.sigmoid(gate_pre)
    hidden = (gate_pre * sigmoid_gate * up_pre).astype(jnp.bfloat16)
    token_rates = (codes.astype(jnp.float32) + 1.0) / 16.0
    target = (-token_rates[:, None] * values.astype(jnp.float32)).astype(jnp.bfloat16)
    back = jnp.dot(target, down_b.T, preferred_element_type=jnp.float32)
    grad_gate_pre = (back * up_pre * sigmoid_gate * (1.0 + gate_pre * (1.0 - sigmoid_gate))).astype(jnp.bfloat16)
    grad_up_pre = (back * gate_pre * sigmoid_gate).astype(jnp.bfloat16)
    grad_gate = jnp.dot(keys.T, grad_gate_pre, preferred_element_type=jnp.float32)
    grad_up = jnp.dot(keys.T, grad_up_pre, preferred_element_type=jnp.float32)
    grad_down = jnp.dot(hidden.T, target, preferred_element_type=jnp.float32)
    new_gate = renew(gate_w, grad_gate).astype(jnp.bfloat16)
    new_up = renew(up_w, grad_up).astype(jnp.bfloat16)
    new_down = renew(down_w, grad_down).astype(jnp.bfloat16)
    query_gate = jnp.dot(queries, new_gate, preferred_element_type=jnp.float32)
    query_up = jnp.dot(queries, new_up, preferred_element_type=jnp.float32)
    query_hidden = (jax.nn.silu(query_gate) * query_up).astype(jnp.bfloat16)
    return jnp.dot(query_hidden, new_down, preferred_element_type=jnp.float32).astype(jnp.bfloat16)

def reference(queries, keys, values, lr_codes, fast_gate, fast_up, fast_down):
    return lax.map(one_head, (queries, keys, values, lr_codes, fast_gate, fast_up, fast_down))
```

```python
import functools

import jax
import jax.numpy as jnp
from jax import lax
from jax.experimental import pallas as pl
from jax.experimental.pallas import tpu as pltpu
from jax.sharding import PartitionSpec as P

EPSILON = 1e-06
STEP_SIZE = 0.5
WIDTH = 2
VMEM_LIMIT = 60 * 1024 * 1024
BF = jnp.bfloat16
F32 = jnp.float32


def place():
    seq = lax.axis_index("seq")
    return lax.div(seq, WIDTH), lax.rem(seq, WIDTH), lax.axis_index("sub")


def device(z, x, s):
    return {"seq": z * WIDTH + x, "sub": s}


def greet(depth, z, x, s):
    barrier = pltpu.get_barrier_semaphore()
    partners = [device(lax.rem(z + k, depth), x, s) for k in range(1, depth)]
    partners += [device(z, 1 - x, s), device(z, x, 1 - s)]
    for partner in partners:
        pl.semaphore_signal(barrier, inc=1, device_id=partner, device_id_type=pl.DeviceIdType.MESH)
    pl.semaphore_wait(barrier, len(partners))


def send(src, dst, send_sem, recv_sem, target):
    return pltpu.make_async_remote_copy(
        src_ref=src,
        dst_ref=dst,
        send_sem=send_sem,
        recv_sem=recv_sem,
        device_id=target,
        device_id_type=pl.DeviceIdType.MESH,
    )


def gather_kernel(depth, own, full, local, zs, zr, xs, xr, cs, cr):
    heads = own.shape[0]
    z, x, s = place()
    greet(depth, z, x, s)
    keep = pltpu.make_async_copy(own, full.at[:, :, z, x, s], local)
    keep.start()

    def along(h, k):
        return send(
            own.at[h],
            full.at[h, :, z, x, s],
            zs.at[h, k - 1],
            zr.at[h, k - 1],
            device(lax.rem(z + k, depth), x, s),
        )

    def across(h):
        block = full.at[h, :, :, x, s]
        return send(block, block, xs.at[h], xr.at[h], device(z, 1 - x, s))

    def inside(h):
        block = full.at[h, :, :, :, s]
        return send(block, block, cs.at[h], cr.at[h], device(z, x, 1 - s))

    def first(h, carry):
        for k in range(1, depth):
            along(h, k).start()
        return carry

    lax.fori_loop(0, heads, first, 0)
    keep.wait()

    def second(h, carry):
        for k in range(1, depth):
            along(h, k).wait_recv()
        across(h).start()

        @pl.when(h > 0)
        def _():
            across(h - 1).wait_recv()
            inside(h - 1).start()

        return carry

    lax.fori_loop(0, heads, second, 0)
    across(heads - 1).wait_recv()
    inside(heads - 1).start()

    def last(h, carry):
        for k in range(1, depth):
            along(h, k).wait_send()
        across(h).wait_send()
        inside(h).wait()
        return carry

    lax.fori_loop(0, heads, last, 0)


def gather(own, depth):
    heads, kinds, rows, cols = own.shape
    dma = pltpu.SemaphoreType.DMA
    full = pl.pallas_call(
        functools.partial(gather_kernel, depth),
        out_shape=jax.ShapeDtypeStruct((heads, kinds, depth, WIDTH, 2, rows, cols), own.dtype),
        in_specs=[pl.BlockSpec(memory_space=pltpu.VMEM)],
        out_specs=pl.BlockSpec(memory_space=pltpu.VMEM),
        scratch_shapes=[
            dma(()),
            dma((heads, depth - 1)),
            dma((heads, depth - 1)),
            dma((heads,)),
            dma((heads,)),
            dma((heads,)),
            dma((heads,)),
        ],
        compiler_params=pltpu.CompilerParams(
            collective_id=0, has_side_effects=True, vmem_limit_bytes=VMEM_LIMIT
        ),
        name="gather",
    )(own)
    return full.reshape(heads, kinds, depth * WIDTH * 2 * rows, cols)


def dot(a, b, dims=((1,), (0,))):
    return lax.dot_general(a, b, (dims, ((), ())), preferred_element_type=F32)


def grads_kernel(keys, values, codes, weights, out):
    tokens, feats = keys.shape[1:]
    half = feats // 2
    rates = (codes[0].astype(F32) + 1.0) / 16.0
    rates = jnp.transpose(jnp.broadcast_to(rates, (128, tokens)))
    rates = jnp.concatenate([rates] * (feats // 128), axis=1)
    target = (-rates * values[0].astype(F32)).astype(BF)
    k = keys[0]
    for j in range(2):
        cols = pl.ds(j * half, half)
        gate_pre = dot(k, weights[0, 0, :, cols])
        up_pre = dot(k, weights[0, 1, :, cols])
        back = dot(target, weights[0, 2, cols, :], ((1,), (1,)))
        sig = jax.nn.sigmoid(gate_pre)
        silu = gate_pre * sig
        hidden = (silu * up_pre).astype(BF)
        ggp = (back * up_pre * sig * (1.0 + gate_pre * (1.0 - sig))).astype(BF)
        gup = (back * silu).astype(BF)
        out[0, j, 0] = dot(k, ggp, ((0,), (0,))).astype(BF)
        out[0, j, 1] = dot(k, gup, ((0,), (0,))).astype(BF)
        down = dot(hidden, target, ((0,), (0,))).astype(BF)
        out[0, 0, 2, cols, :] = down[:, :half]
        out[0, 1, 2, cols, :] = down[:, half:]


def local_grads(keys, values, codes, weights):
    heads, tokens, feats = keys.shape
    block = pl.BlockSpec((1, tokens, feats), lambda h: (h, 0, 0))
    return pl.pallas_call(
        grads_kernel,
        grid=(heads,),
        out_shape=jax.ShapeDtypeStruct((heads, 2, 3, feats, feats // 2), BF),
        in_specs=[
            block,
            block,
            pl.BlockSpec((1, 1, tokens), lambda h: (h, 0, 0)),
            pl.BlockSpec((1, 3, feats, feats), lambda h: (h, 0, 0, 0)),
        ],
        out_specs=pl.BlockSpec((1, 2, 3, feats, feats // 2), lambda h: (h, 0, 0, 0, 0)),
        compiler_params=pltpu.CompilerParams(vmem_limit_bytes=VMEM_LIMIT),
        name="grads",
    )(keys, values, codes[:, None, :], weights)


def apply_kernel(queries, weights, out):
    q = queries[0]
    half = weights.shape[-1]
    total = [None, None]
    for j in range(2):
        gate = dot(q, weights[0, j, 0])
        up = dot(q, weights[0, j, 1])
        hidden = (gate * jax.nn.sigmoid(gate) * up).astype(BF)
        for c in range(2):
            term = dot(hidden, weights[0, c, 2, pl.ds(j * half, half), :])
            total[c] = term if j == 0 else total[c] + term
    for c in range(2):
        out[0, :, pl.ds(c * half, half)] = total[c].astype(BF)


def apply_fast(queries, weights):
    heads, tokens, feats = queries.shape
    block = pl.BlockSpec((1, tokens, feats), lambda h: (h, 0, 0))
    return pl.pallas_call(
        apply_kernel,
        grid=(heads,),
        out_shape=jax.ShapeDtypeStruct(queries.shape, BF),
        in_specs=[
            block,
            pl.BlockSpec((1, 2, 3, feats, feats // 2), lambda h: (h, 0, 0, 0, 0)),
        ],
        out_specs=block,
        compiler_params=pltpu.CompilerParams(vmem_limit_bytes=VMEM_LIMIT),
        name="apply",
    )(queries, weights)


def renew_kernel(
    depth, grads, weights, new, paired, summed, got_c, got_x, got_z, total, norm_out, norm_in,
    cs, cr, xs, xr, zs, zr, ns, nr, azs, azr, axs, axr, acs, acr,
):
    kinds, rows, half = grads.shape[2:]
    z, x, s = place()
    greet(depth, z, x, s)

    def row(k):
        return lax.rem(z + k, depth)

    def inside(zt, xt):
        head = zt * WIDTH + xt
        return send(
            grads.at[head, 1 - s], got_c.at[head], cs.at[head], cr.at[head], device(z, x, 1 - s)
        )

    def across(k):
        return send(paired.at[k], got_x.at[k], xs.at[k], xr.at[k], device(z, 1 - x, s))

    def along(k):
        return send(
            summed.at[k - 1], got_z.at[k - 1], zs.at[k - 1], zr.at[k - 1], device(row(k), x, s)
        )

    order = [k for k in range(1, depth)] + [0]
    for xt in (1 - x, x):
        for k in order:
            inside(row(k), xt).start()
    for k in order:
        head = row(k) * WIDTH + 1 - x
        inside(row(k), 1 - x).wait_recv()
        for m in range(kinds):
            paired[k, m] = (grads[head, s, m].astype(F32) + got_c[head, m].astype(F32)).astype(BF)
        across(k).start()
    for k in order:
        head = row(k) * WIDTH + x
        inside(row(k), x).wait_recv()
        across(k).wait_recv()
        if k > 0:
            for m in range(kinds):
                both = grads[head, s, m].astype(F32) + got_c[head, m].astype(F32)
                summed[k - 1, m] = (both + got_x[k, m].astype(F32)).astype(BF)
            along(k).start()
    for k in range(1, depth):
        along(k).wait_recv()
    mine = z * WIDTH + x
    for m in range(kinds):
        part = grads[mine, s, m].astype(F32) + got_c[mine, m].astype(F32)
        part = part + got_x[0, m].astype(F32)
        for k in range(1, depth):
            part = part + got_z[k - 1, m].astype(F32)
        total[m] = part
        norm_out[m] = jnp.broadcast_to(jnp.sum(part * part, keepdims=True), norm_out.shape[1:])
    norms = send(norm_out, norm_in, ns, nr, device(z, x, 1 - s))
    norms.start()
    norms.wait()

    def share_z(m, k):
        block = new.at[z, x, s, m]
        return send(block, block, azs.at[m, k - 1], azr.at[m, k - 1], device(row(k), x, s))

    def share_x(m, k):
        block = new.at[lax.rem(z + depth - k, depth), x, s, m]
        return send(block, block, axs.at[m, k], axr.at[m, k], device(z, 1 - x, s))

    def share_c(m):
        block = new.at[:, :, s, m]
        return send(block, block, acs.at[m], acr.at[m], device(z, x, 1 - s))

    for m in range(kinds):
        whole = weights[m].astype(F32)
        weight_total = jnp.sum(whole * whole, keepdims=True)
        grad_total = norm_out[m, :1, :1] + norm_in[m, :1, :1]
        scale = STEP_SIZE * jnp.sqrt(weight_total + EPSILON) / jnp.sqrt(grad_total + EPSILON)
        own = weights[m, :, pl.ds(pl.multiple_of(s * half, half), half)].astype(F32)
        moved = own - scale * total[m]
        col_weight = jnp.sum(own * own, axis=0, keepdims=True)
        col_moved = jnp.sum(moved * moved, axis=0, keepdims=True)
        ratio = jnp.sqrt((col_weight + EPSILON) / (col_moved + EPSILON))
        new[z, x, s, m] = (moved * ratio).astype(BF)
        for k in range(1, depth):
            share_z(m, k).start()
        share_x(m, 0).start()
    for m in range(kinds):
        for k in range(1, depth):
            share_z(m, k).wait_recv()
            share_x(m, k).start()
        if m > 0:
            for k in range(depth):
                share_x(m - 1, k).wait_recv()
            share_c(m - 1).start()
    for k in range(depth):
        share_x(kinds - 1, k).wait_recv()
    share_c(kinds - 1).start()

    for xt in (1 - x, x):
        for k in order:
            inside(row(k), xt).wait_send()
    for k in order:
        across(k).wait_send()
    for k in range(1, depth):
        along(k).wait_send()
    for m in range(kinds):
        for k in range(depth):
            if k > 0:
                share_z(m, k).wait_send()
            share_x(m, k).wait_send()
        share_c(m).wait()


def renew(grads, weights, depth):
    heads, _, kinds, rows, half = grads.shape
    dma = pltpu.SemaphoreType.DMA
    piece = (kinds, rows, half)
    new = pl.pallas_call(
        functools.partial(renew_kernel, depth),
        out_shape=jax.ShapeDtypeStruct((depth, WIDTH, 2) + piece, BF),
        in_specs=[pl.BlockSpec(memory_space=pltpu.VMEM)] * 2,
        out_specs=pl.BlockSpec(memory_space=pltpu.VMEM),
        scratch_shapes=[
            pltpu.VMEM((depth,) + piece, BF),
            pltpu.VMEM((depth - 1,) + piece, BF),
            pltpu.VMEM((heads,) + piece, BF),
            pltpu.VMEM((depth,) + piece, BF),
            pltpu.VMEM((depth - 1,) + piece, BF),
            pltpu.VMEM(piece, F32),
            pltpu.VMEM((kinds, 8, 128), F32),
            pltpu.VMEM((kinds, 8, 128), F32),
            dma((heads,)),
            dma((heads,)),
            dma((depth,)),
            dma((depth,)),
            dma((depth - 1,)),
            dma((depth - 1,)),
            dma(()),
            dma(()),
            dma((kinds, depth - 1)),
            dma((kinds, depth - 1)),
            dma((kinds, depth)),
            dma((kinds, depth)),
            dma((kinds,)),
            dma((kinds,)),
        ],
        compiler_params=pltpu.CompilerParams(
            collective_id=1, has_side_effects=True, vmem_limit_bytes=VMEM_LIMIT
        ),
        name="renew",
    )(grads, weights)
    return new.reshape((heads, 2) + piece)


def on_device_heads(depth, queries, keys, values, lr_codes, fast_gate, fast_up, fast_down):
    own = jnp.stack([fast_gate, fast_up, fast_down], axis=1).astype(BF)
    weights = gather(own, depth)
    grads = local_grads(keys, values, lr_codes, weights)
    mine = lax.dynamic_index_in_dim(weights, lax.axis_index("seq"), 0, keepdims=False)
    new = renew(grads, mine, depth)
    return apply_fast(queries, new)


def column_squares(matrix):
    return jnp.sum(matrix * matrix, axis=1)


def rescale(moved, col_weight, col_moved):
    return moved * jnp.sqrt((col_weight + EPSILON) / (col_moved + EPSILON))[:, None, :]


def step_scale(col_weight, grad_total):
    return (
        STEP_SIZE * jnp.sqrt(jnp.sum(col_weight, axis=1) + EPSILON) / jnp.sqrt(grad_total + EPSILON)
    )


def apply_rows(queries, gate_b, up_b, down_b):
    query_gate = jnp.einsum("htd,hdf->htf", queries, gate_b, preferred_element_type=jnp.float32)
    query_up = jnp.einsum("htd,hdf->htf", queries, up_b, preferred_element_type=jnp.float32)
    query_hidden = (jax.nn.silu(query_gate) * query_up).astype(jnp.bfloat16)
    return jnp.einsum(
        "htf,hfd->htd", query_hidden, down_b, preferred_element_type=jnp.float32
    ).astype(jnp.bfloat16)


def local_grads_rows(keys, target, gate_b, up_b, down_b):
    gate_pre = jnp.einsum("htd,hdf->htf", keys, gate_b, preferred_element_type=jnp.float32)
    up_pre = jnp.einsum("htd,hdf->htf", keys, up_b, preferred_element_type=jnp.float32)
    sigmoid_gate = jax.nn.sigmoid(gate_pre)
    hidden = (gate_pre * sigmoid_gate * up_pre).astype(jnp.bfloat16)
    back = jnp.einsum("htd,hfd->htf", target, down_b, preferred_element_type=jnp.float32)
    grad_gate_pre = (back * up_pre * sigmoid_gate * (1.0 + gate_pre * (1.0 - sigmoid_gate))).astype(
        jnp.bfloat16
    )
    grad_up_pre = (back * gate_pre * sigmoid_gate).astype(jnp.bfloat16)
    grad_gate = jnp.einsum("htd,htf->hdf", keys, grad_gate_pre, preferred_element_type=jnp.float32)
    grad_up = jnp.einsum("htd,htf->hdf", keys, grad_up_pre, preferred_element_type=jnp.float32)
    grad_down = jnp.einsum("htf,htd->hfd", hidden, target, preferred_element_type=jnp.float32)
    return (grad_gate, grad_up, grad_down)


def on_device_rows(queries, keys, values, lr_codes, fast_gate, fast_up, fast_down):
    token_rates = (lr_codes.astype(jnp.float32) + 1.0) / 16.0
    target = (-token_rates[:, :, None] * values.astype(jnp.float32)).astype(jnp.bfloat16)
    gate_b, up_b, down_b = (
        lax.all_gather(fast_gate.astype(jnp.bfloat16), ("seq", "sub"), axis=1, tiled=True),
        lax.all_gather(fast_up.astype(jnp.bfloat16), ("seq", "sub"), axis=1, tiled=True),
        lax.all_gather(fast_down.astype(jnp.bfloat16), ("seq", "sub"), axis=1, tiled=True),
    )
    grad_gate, grad_up, grad_down = local_grads_rows(keys, target, gate_b, up_b, down_b)
    owned = (
        lax.psum_scatter(grad_gate, ("seq", "sub"), scatter_dimension=1, tiled=True),
        lax.psum_scatter(grad_up, ("seq", "sub"), scatter_dimension=1, tiled=True),
        lax.psum_scatter(grad_down, ("seq", "sub"), scatter_dimension=1, tiled=True),
    )
    weights = (fast_gate, fast_up, fast_down)
    grad_local = jnp.stack(
        [
            jnp.sum(owned[0] * owned[0], axis=(1, 2)),
            jnp.sum(owned[1] * owned[1], axis=(1, 2)),
            jnp.sum(owned[2] * owned[2], axis=(1, 2)),
        ],
        axis=1,
    )
    col_gate, col_up, col_down, grad_totals = lax.psum(
        (column_squares(fast_gate), column_squares(fast_up), column_squares(fast_down), grad_local),
        ("seq", "sub"),
    )
    col_weights = (col_gate, col_up, col_down)
    moved_all = []
    for index in range(3):
        scale = step_scale(col_weights[index], grad_totals[:, index])
        moved_all.append(weights[index] - scale[:, None, None] * owned[index])
    moved_cols = lax.psum(
        (column_squares(moved_all[0]), column_squares(moved_all[1]), column_squares(moved_all[2])),
        ("seq", "sub"),
    )
    renewed = [
        rescale(moved_all[index], col_weights[index], moved_cols[index]).astype(jnp.bfloat16)
        for index in range(3)
    ]
    new_gate, new_up, new_down = (
        lax.all_gather(renewed[0], ("seq", "sub"), axis=1, tiled=True),
        lax.all_gather(renewed[1], ("seq", "sub"), axis=1, tiled=True),
        lax.all_gather(renewed[2], ("seq", "sub"), axis=1, tiled=True),
    )
    return apply_rows(queries, new_gate, new_up, new_down)


def solution(mesh):
    seq, sub = mesh.shape["seq"], mesh.shape["sub"]

    def on_device(*arrays):
        if sub == 2 and seq % WIDTH == 0 and seq > WIDTH and arrays[4].shape[0] == seq:
            return on_device_heads(seq // WIDTH, *arrays)
        return on_device_rows(*arrays)

    return jax.shard_map(
        on_device,
        mesh=mesh,
        in_specs=(
            P("head", ("groups", "seq", "sub"), None),
            P("head", ("groups", "seq", "sub"), None),
            P("head", ("groups", "seq", "sub"), None),
            P("head", ("groups", "seq", "sub")),
            P("head", ("seq", "sub"), None),
            P("head", ("seq", "sub"), None),
            P("head", ("seq", "sub"), None),
        ),
        out_specs=P("head", ("groups", "seq", "sub"), None),
        check_vma=False,
    )
```

```python
import functools

import jax
import jax.numpy as jnp
from jax import lax
from jax.experimental import pallas as pl
from jax.experimental.pallas import tpu as pltpu
from jax.sharding import PartitionSpec as P

EPSILON = 1e-06
STEP_SIZE = 0.5
KIND = (0, 2, 1)
WIDTH = 2
VMEM_LIMIT = 60 * 1024 * 1024
BF = jnp.bfloat16
F32 = jnp.float32


def place():
    seq = lax.axis_index("seq")
    return lax.div(seq, WIDTH), lax.rem(seq, WIDTH), lax.axis_index("sub")


def device(z, x, s):
    return {"seq": z * WIDTH + x, "sub": s}


def greet(depth, z, x, s, others=()):
    barrier = pltpu.get_barrier_semaphore()
    partners = [device(lax.rem(z + k, depth), x, s) for k in range(1, depth)]
    partners += [device(z, 1 - x, s), device(z, x, 1 - s), *others]
    for partner in partners:
        pl.semaphore_signal(barrier, inc=1, device_id=partner, device_id_type=pl.DeviceIdType.MESH)
    pl.semaphore_wait(barrier, len(partners))


def send(src, dst, send_sem, recv_sem, target):
    return pltpu.make_async_remote_copy(
        src_ref=src,
        dst_ref=dst,
        send_sem=send_sem,
        recv_sem=recv_sem,
        device_id=target,
        device_id_type=pl.DeviceIdType.MESH,
    )


def dot(a, b, dims=((1,), (0,))):
    return lax.dot_general(a, b, (dims, ((), ())), preferred_element_type=F32)


def chain(depth, z, hop, started, unit, k):
    for back in (True, False):
        src = z - k if back else z + k
        onward = 1 if back else -1
        here = (src >= 0) if back else (src < depth)

        @pl.when(here)
        def _(src=src, onward=onward):
            hop(unit, src, -onward).wait_recv()
            started(unit, src)

            @pl.when((z + onward >= 0) & (z + onward < depth))
            def _():
                hop(unit, src, onward).start()


def chain_own(depth, z, hop, unit):
    for onward in (1, -1):

        @pl.when((z + onward >= 0) & (z + onward < depth))
        def _(onward=onward):
            hop(unit, z, onward).start()


def chain_sent(depth, z, hop, unit):
    for src in range(depth):

        @pl.when((src <= z) & (z < depth - 1))
        def _(src=src):
            hop(unit, src, 1).wait_send()

        @pl.when((src >= z) & (z > 0))
        def _(src=src):
            hop(unit, src, -1).wait_send()


def head_grads(k, values, codes, full, h, out):
    tokens, feats = k.shape
    half = feats // 2
    depth = full.shape[2]
    rates = (codes.astype(F32) + 1.0) / 16.0
    rates = jnp.transpose(jnp.broadcast_to(rates, (128, tokens)))
    rates = jnp.concatenate([rates] * (feats // 128), axis=1)
    target = (-rates * values.astype(F32)).astype(BF)
    for j in range(2):
        cols = pl.ds(j * half, half)
        gate = full[h, 0, :, :, :, :, cols].reshape(feats, half)
        up = full[h, 2, :, :, :, :, cols].reshape(feats, half)
        down = full[h, 1, pl.ds(j * (depth // 2), depth // 2)].reshape(half, feats)
        gate_pre = dot(k, gate)
        up_pre = dot(k, up)
        back = dot(target, down, ((1,), (1,)))
        sig = jax.nn.sigmoid(gate_pre)
        silu = gate_pre * sig
        hidden = (silu * up_pre).astype(BF)
        ggp = (back * up_pre * sig * (1.0 + gate_pre * (1.0 - sig))).astype(BF)
        gup = (back * silu).astype(BF)
        out[j, 0] = dot(k, ggp, ((0,), (0,))).astype(BF)
        out[j, 1] = dot(k, gup, ((0,), (0,))).astype(BF)
        gdown = dot(hidden, target, ((0,), (0,))).astype(BF)
        out[0, 2, cols, :] = gdown[:, :half]
        out[1, 2, cols, :] = gdown[:, half:]


def gather_kernel(
    depth, own, keys, values, codes, grads, mine, full, kbuf, vbuf, obuf,
    local, ksem, vsem, osem, sr, sl, zr, xs, xr, ys, yr, cs, cr,
):
    heads = own.shape[0]
    z, x, s = place()
    y = lax.axis_index("groups")

    def load(h):
        slot = lax.rem(h, 2)
        return (
            pltpu.make_async_copy(keys.at[h], kbuf.at[slot], ksem.at[slot]),
            pltpu.make_async_copy(values.at[h], vbuf.at[slot], vsem.at[slot]),
        )

    def store(h):
        slot = lax.rem(h, 2)
        return pltpu.make_async_copy(obuf.at[slot], grads.at[h], osem.at[slot])

    for copy in load(0) + load(1):
        copy.start()
    pair = pl.ds(y, 2)
    keep = pltpu.make_async_copy(own.at[:, pair], full.at[:, pair, z, x, s], local)
    keep.start()
    greet(depth, z, x, s, ({"groups": 1 - y},))
    keep.wait()

    def hop(h, src, onward):
        block = full.at[h, pair, src, x, s]
        sems = sr if onward == 1 else sl
        return send(block, block, sems.at[h, src], zr.at[h, src], device(z + onward, x, s))

    def across(h, src):
        block = full.at[h, pair, src, x, s]
        return send(block, block, xs.at[h, src], xr.at[h, src], device(z, 1 - x, s))

    def over(h):
        block = full.at[h, 2 * y, :, :, s]
        return send(block, block, ys.at[h], yr.at[h], {"groups": 1 - y})

    def inside(h):
        block = full.at[h, :, :, :, s]
        return send(block, block, cs.at[h], cr.at[h], device(z, x, 1 - s))

    def first(h):
        chain_own(depth, z, hop, h)
        across(h, z).start()

    def hand(h):
        for src in range(depth):
            across(h, src).wait_recv()
        over(h).start()

    def spread(h):
        over(h).wait_recv()
        inside(h).start()

    def compute(h):
        slot = lax.rem(h, 2)
        inside(h).wait_recv()
        for copy in load(h):
            copy.wait()

        @pl.when(h >= 2)
        def _():
            store(h - 2).wait()

        head_grads(kbuf[slot], vbuf[slot], codes[h], full, h, obuf.at[slot])
        store(h).start()

        @pl.when(h + 2 < heads)
        def _():
            for copy in load(h + 2):
                copy.start()

    ahead = 2
    for h in range(ahead):
        first(h)

    def step(t, carry):
        def when(h, what):
            pl.when((h >= 0) & (h < heads))(lambda: what(h))

        when(t + ahead, first)
        when(t - depth, spread)
        when(t - depth + 1, hand)
        for k in range(depth - 1, 0, -1):
            when(t - k + 1, lambda h, k=k: chain(depth, z, hop, lambda u, i: across(u, i).start(), h, k))
        when(t - depth - 1, compute)
        return carry

    lax.fori_loop(0, heads + depth + 1, step, 0)
    feats = mine.shape[1]
    for m in range(3):
        mine[m] = full[z * WIDTH + x, m].reshape(feats, feats)

    def last(h, carry):
        chain_sent(depth, z, hop, h)
        for src in range(depth):
            across(h, src).wait_send()
        over(h).wait_send()
        inside(h).wait_send()
        return carry

    lax.fori_loop(0, heads, last, 0)
    store(heads - 2).wait()
    store(heads - 1).wait()


def gather_grads(own, keys, values, codes, depth):
    heads, kinds, rows, cols = own.shape
    tokens, feats = keys.shape[1:]
    dma = pltpu.SemaphoreType.DMA
    vmem = pl.BlockSpec(memory_space=pltpu.VMEM)
    anywhere = pl.BlockSpec(memory_space=pl.ANY)
    block = (2, kinds, feats, feats // 2)
    return pl.pallas_call(
        functools.partial(gather_kernel, depth),
        out_shape=(
            jax.ShapeDtypeStruct((heads,) + block, BF),
            jax.ShapeDtypeStruct((kinds, feats, feats), BF),
        ),
        in_specs=[vmem, anywhere, anywhere, vmem],
        out_specs=(anywhere, vmem),
        scratch_shapes=[
            pltpu.VMEM((heads, kinds, depth, WIDTH, 2, rows, cols), BF),
            pltpu.VMEM((2, tokens, feats), BF),
            pltpu.VMEM((2, tokens, feats), BF),
            pltpu.VMEM((2,) + block, BF),
            dma(()),
            dma((2,)),
            dma((2,)),
            dma((2,)),
            *[dma((heads, depth))] * 5,
            *[dma((heads,))] * 4,
        ],
        compiler_params=pltpu.CompilerParams(
            collective_id=0, has_side_effects=True, vmem_limit_bytes=VMEM_LIMIT
        ),
        name="gather_grads",
    )(own, keys, values, codes[:, None, :])


def apply_kernel(queries, weights, out):
    q = queries[0]
    half = weights.shape[-1]
    total = [None, None]
    for j in range(2):
        gate = dot(q, weights[0, j, 0])
        up = dot(q, weights[0, j, 1])
        hidden = (gate * jax.nn.sigmoid(gate) * up).astype(BF)
        for c in range(2):
            term = dot(hidden, weights[0, c, 2, pl.ds(j * half, half), :])
            total[c] = term if j == 0 else total[c] + term
    for c in range(2):
        out[0, :, pl.ds(c * half, half)] = total[c].astype(BF)


def apply_fast(queries, weights):
    heads, tokens, feats = queries.shape
    block = pl.BlockSpec((1, tokens, feats), lambda h: (h, 0, 0))
    return pl.pallas_call(
        apply_kernel,
        grid=(heads,),
        out_shape=jax.ShapeDtypeStruct(queries.shape, BF),
        in_specs=[
            block,
            pl.BlockSpec((1, 2, 3, feats, feats // 2), lambda h: (h, 0, 0, 0, 0)),
        ],
        out_specs=block,
        compiler_params=pltpu.CompilerParams(vmem_limit_bytes=VMEM_LIMIT),
        name="apply",
    )(queries, weights)


def renew_kernel(
    depth, grads, weights, new, paired, summed, got_c, got_x, got_z, total, norm_out, norm_in,
    cs, cr, xs, xr, zs, zr, ns, nr, asr, asl, azr, axs, axr, acs, acr,
):
    kinds, rows, half = grads.shape[2:]
    z, x, s = place()
    greet(depth, z, x, s)

    def row(k):
        return lax.rem(z + k, depth)

    def inside(zt, xt):
        head = zt * WIDTH + xt
        return send(
            grads.at[head, 1 - s], got_c.at[head], cs.at[head], cr.at[head], device(z, x, 1 - s)
        )

    def across(k):
        return send(paired.at[k], got_x.at[k], xs.at[k], xr.at[k], device(z, 1 - x, s))

    def along(k):
        return send(
            summed.at[k - 1], got_z.at[k - 1], zs.at[k - 1], zr.at[k - 1], device(row(k), x, s)
        )

    order = [k for k in range(1, depth)] + [0]
    for xt in (1 - x, x):
        for k in order:
            inside(row(k), xt).start()
    for k in order:
        head = row(k) * WIDTH + 1 - x
        inside(row(k), 1 - x).wait_recv()
        for m in range(kinds):
            paired[k, m] = (grads[head, s, m].astype(F32) + got_c[head, m].astype(F32)).astype(BF)
        across(k).start()
    for k in order:
        head = row(k) * WIDTH + x
        inside(row(k), x).wait_recv()
        across(k).wait_recv()
        if k > 0:
            for m in range(kinds):
                both = grads[head, s, m].astype(F32) + got_c[head, m].astype(F32)
                summed[k - 1, m] = (both + got_x[k, m].astype(F32)).astype(BF)
            along(k).start()
    for k in range(1, depth):
        along(k).wait_recv()
    mine = z * WIDTH + x
    for m in range(kinds):
        part = grads[mine, s, m].astype(F32) + got_c[mine, m].astype(F32)
        part = part + got_x[0, m].astype(F32)
        for k in range(1, depth):
            part = part + got_z[k - 1, m].astype(F32)
        total[m] = part
        norm_out[m] = jnp.broadcast_to(jnp.sum(part * part, keepdims=True), norm_out.shape[1:])
    norms = send(norm_out, norm_in, ns, nr, device(z, x, 1 - s))
    norms.start()
    norms.wait()

    def hop(m, src, onward):
        block = new.at[src, x, s, m]
        sems = asr if onward == 1 else asl
        return send(block, block, sems.at[m, src], azr.at[m, src], device(z + onward, x, s))

    def share_x(m, src):
        block = new.at[src, x, s, m]
        return send(block, block, axs.at[m, src], axr.at[m, src], device(z, 1 - x, s))

    def share_c(m, src):
        block = new.at[src, :, s, m]
        return send(block, block, acs.at[m, src], acr.at[m, src], device(z, x, 1 - s))

    def pass_on(m, src):
        share_x(m, src).wait_recv()
        share_c(m, src).start()

    for m in range(kinds):
        whole = weights[KIND[m]].astype(F32)
        weight_total = jnp.sum(whole * whole, keepdims=True)
        grad_total = norm_out[m, :1, :1] + norm_in[m, :1, :1]
        scale = STEP_SIZE * jnp.sqrt(weight_total + EPSILON) / jnp.sqrt(grad_total + EPSILON)
        own = weights[KIND[m], :, pl.ds(pl.multiple_of(s * half, half), half)].astype(F32)
        moved = own - scale * total[m]
        col_weight = jnp.sum(own * own, axis=0, keepdims=True)
        col_moved = jnp.sum(moved * moved, axis=0, keepdims=True)
        ratio = jnp.sqrt((col_weight + EPSILON) / (col_moved + EPSILON))
        new[z, x, s, m] = (moved * ratio).astype(BF)
        chain_own(depth, z, hop, m)
        share_x(m, z).start()
    for k in range(1, depth + 1):
        for m in range(kinds):
            if k < depth:
                chain(depth, z, hop, lambda u, i: share_x(u, i).start(), m, k)
            if k == 1:
                pass_on(m, z)
            else:
                pl.when(z - k + 1 >= 0)(lambda m=m, k=k: pass_on(m, z - k + 1))
                pl.when(z + k - 1 < depth)(lambda m=m, k=k: pass_on(m, z + k - 1))

    for xt in (1 - x, x):
        for k in order:
            inside(row(k), xt).wait_send()
    for k in order:
        across(k).wait_send()
    for k in range(1, depth):
        along(k).wait_send()
    for m in range(kinds):
        chain_sent(depth, z, hop, m)
        for src in range(depth):
            share_x(m, src).wait_send()
            share_c(m, src).wait()


def renew(grads, weights, depth):
    heads, _, kinds, rows, half = grads.shape
    dma = pltpu.SemaphoreType.DMA
    piece = (kinds, rows, half)
    new = pl.pallas_call(
        functools.partial(renew_kernel, depth),
        out_shape=jax.ShapeDtypeStruct((depth, WIDTH, 2) + piece, BF),
        in_specs=[pl.BlockSpec(memory_space=pltpu.VMEM)] * 2,
        out_specs=pl.BlockSpec(memory_space=pltpu.VMEM),
        scratch_shapes=[
            pltpu.VMEM((depth,) + piece, BF),
            pltpu.VMEM((depth - 1,) + piece, BF),
            pltpu.VMEM((heads,) + piece, BF),
            pltpu.VMEM((depth,) + piece, BF),
            pltpu.VMEM((depth - 1,) + piece, BF),
            pltpu.VMEM(piece, F32),
            pltpu.VMEM((kinds, 8, 128), F32),
            pltpu.VMEM((kinds, 8, 128), F32),
            dma((heads,)),
            dma((heads,)),
            dma((depth,)),
            dma((depth,)),
            dma((depth - 1,)),
            dma((depth - 1,)),
            dma(()),
            dma(()),
            *[dma((kinds, depth))] * 7,
        ],
        compiler_params=pltpu.CompilerParams(
            collective_id=1, has_side_effects=True, vmem_limit_bytes=VMEM_LIMIT
        ),
        name="renew",
    )(grads, weights)
    return new.reshape((heads, 2) + piece)


def on_device_heads(depth, queries, keys, values, lr_codes, fast_gate, fast_up, fast_down):
    own = jnp.stack([fast_gate, fast_down, fast_up], axis=1).astype(BF)
    grads, mine = gather_grads(own, keys, values, lr_codes, depth)
    new = renew(grads, mine, depth)
    return apply_fast(queries, new)


def column_squares(matrix):
    return jnp.sum(matrix * matrix, axis=1)


def rescale(moved, col_weight, col_moved):
    return moved * jnp.sqrt((col_weight + EPSILON) / (col_moved + EPSILON))[:, None, :]


def step_scale(col_weight, grad_total):
    return (
        STEP_SIZE * jnp.sqrt(jnp.sum(col_weight, axis=1) + EPSILON) / jnp.sqrt(grad_total + EPSILON)
    )


def apply_rows(queries, gate_b, up_b, down_b):
    query_gate = jnp.einsum("htd,hdf->htf", queries, gate_b, preferred_element_type=jnp.float32)
    query_up = jnp.einsum("htd,hdf->htf", queries, up_b, preferred_element_type=jnp.float32)
    query_hidden = (jax.nn.silu(query_gate) * query_up).astype(jnp.bfloat16)
    return jnp.einsum(
        "htf,hfd->htd", query_hidden, down_b, preferred_element_type=jnp.float32
    ).astype(jnp.bfloat16)


def local_grads_rows(keys, target, gate_b, up_b, down_b):
    gate_pre = jnp.einsum("htd,hdf->htf", keys, gate_b, preferred_element_type=jnp.float32)
    up_pre = jnp.einsum("htd,hdf->htf", keys, up_b, preferred_element_type=jnp.float32)
    sigmoid_gate = jax.nn.sigmoid(gate_pre)
    hidden = (gate_pre * sigmoid_gate * up_pre).astype(jnp.bfloat16)
    back = jnp.einsum("htd,hfd->htf", target, down_b, preferred_element_type=jnp.float32)
    grad_gate_pre = (back * up_pre * sigmoid_gate * (1.0 + gate_pre * (1.0 - sigmoid_gate))).astype(
        jnp.bfloat16
    )
    grad_up_pre = (back * gate_pre * sigmoid_gate).astype(jnp.bfloat16)
    grad_gate = jnp.einsum("htd,htf->hdf", keys, grad_gate_pre, preferred_element_type=jnp.float32)
    grad_up = jnp.einsum("htd,htf->hdf", keys, grad_up_pre, preferred_element_type=jnp.float32)
    grad_down = jnp.einsum("htf,htd->hfd", hidden, target, preferred_element_type=jnp.float32)
    return (grad_gate, grad_up, grad_down)


def on_device_rows(queries, keys, values, lr_codes, fast_gate, fast_up, fast_down):
    token_rates = (lr_codes.astype(jnp.float32) + 1.0) / 16.0
    target = (-token_rates[:, :, None] * values.astype(jnp.float32)).astype(jnp.bfloat16)
    gate_b, up_b, down_b = (
        lax.all_gather(fast_gate.astype(jnp.bfloat16), ("seq", "sub"), axis=1, tiled=True),
        lax.all_gather(fast_up.astype(jnp.bfloat16), ("seq", "sub"), axis=1, tiled=True),
        lax.all_gather(fast_down.astype(jnp.bfloat16), ("seq", "sub"), axis=1, tiled=True),
    )
    grad_gate, grad_up, grad_down = local_grads_rows(keys, target, gate_b, up_b, down_b)
    owned = (
        lax.psum_scatter(grad_gate, ("seq", "sub"), scatter_dimension=1, tiled=True),
        lax.psum_scatter(grad_up, ("seq", "sub"), scatter_dimension=1, tiled=True),
        lax.psum_scatter(grad_down, ("seq", "sub"), scatter_dimension=1, tiled=True),
    )
    weights = (fast_gate, fast_up, fast_down)
    grad_local = jnp.stack(
        [
            jnp.sum(owned[0] * owned[0], axis=(1, 2)),
            jnp.sum(owned[1] * owned[1], axis=(1, 2)),
            jnp.sum(owned[2] * owned[2], axis=(1, 2)),
        ],
        axis=1,
    )
    col_gate, col_up, col_down, grad_totals = lax.psum(
        (column_squares(fast_gate), column_squares(fast_up), column_squares(fast_down), grad_local),
        ("seq", "sub"),
    )
    col_weights = (col_gate, col_up, col_down)
    moved_all = []
    for index in range(3):
        scale = step_scale(col_weights[index], grad_totals[:, index])
        moved_all.append(weights[index] - scale[:, None, None] * owned[index])
    moved_cols = lax.psum(
        (column_squares(moved_all[0]), column_squares(moved_all[1]), column_squares(moved_all[2])),
        ("seq", "sub"),
    )
    renewed = [
        rescale(moved_all[index], col_weights[index], moved_cols[index]).astype(jnp.bfloat16)
        for index in range(3)
    ]
    new_gate, new_up, new_down = (
        lax.all_gather(renewed[0], ("seq", "sub"), axis=1, tiled=True),
        lax.all_gather(renewed[1], ("seq", "sub"), axis=1, tiled=True),
        lax.all_gather(renewed[2], ("seq", "sub"), axis=1, tiled=True),
    )
    return apply_rows(queries, new_gate, new_up, new_down)


def solution(mesh):
    groups, seq, sub = (mesh.shape[axis] for axis in ("groups", "seq", "sub"))

    def on_device(*arrays):
        if groups == 2 and sub == 2 and seq % (2 * WIDTH) == 0 and arrays[4].shape[0] == seq:
            return on_device_heads(seq // WIDTH, *arrays)
        return on_device_rows(*arrays)

    return jax.shard_map(
        on_device,
        mesh=mesh,
        in_specs=(
            P("head", ("groups", "seq", "sub"), None),
            P("head", ("groups", "seq", "sub"), None),
            P("head", ("groups", "seq", "sub"), None),
            P("head", ("groups", "seq", "sub")),
            P("head", ("seq", "sub"), None),
            P("head", ("seq", "sub"), None),
            P("head", ("seq", "sub"), None),
        ),
        out_specs=P("head", ("groups", "seq", "sub"), None),
        check_vma=False,
    )
```

```python
import functools

import jax
import jax.numpy as jnp
from jax import lax
from jax.experimental import pallas as pl
from jax.experimental.pallas import tpu as pltpu
from jax.sharding import PartitionSpec as P

EPSILON = 1e-06
STEP_SIZE = 0.5
KIND = (0, 2, 1)
WIDTH = 2
VMEM_LIMIT = 60 * 1024 * 1024
BF = jnp.bfloat16
F32 = jnp.float32


def place():
    seq = lax.axis_index("seq")
    return lax.div(seq, WIDTH), lax.rem(seq, WIDTH), lax.axis_index("sub")


def device(z, x, s):
    return {"seq": z * WIDTH + x, "sub": s}


def greet(depth, z, x, s, others=()):
    barrier = pltpu.get_barrier_semaphore()
    partners = [device(lax.rem(z + k, depth), x, s) for k in range(1, depth)]
    partners += [device(z, 1 - x, s), device(z, x, 1 - s), *others]
    for partner in partners:
        pl.semaphore_signal(barrier, inc=1, device_id=partner, device_id_type=pl.DeviceIdType.MESH)
    pl.semaphore_wait(barrier, len(partners))


def send(src, dst, send_sem, recv_sem, target):
    return pltpu.make_async_remote_copy(
        src_ref=src,
        dst_ref=dst,
        send_sem=send_sem,
        recv_sem=recv_sem,
        device_id=target,
        device_id_type=pl.DeviceIdType.MESH,
    )


def dot(a, b, dims=((1,), (0,))):
    return lax.dot_general(a, b, (dims, ((), ())), preferred_element_type=F32)


def chain(depth, z, hop, started, unit, k):
    for back in (True, False):
        src = z - k if back else z + k
        onward = 1 if back else -1
        here = (src >= 0) if back else (src < depth)

        @pl.when(here)
        def _(src=src, onward=onward):
            hop(unit, src, -onward).wait_recv()
            started(unit, src)

            @pl.when((z + onward >= 0) & (z + onward < depth))
            def _():
                hop(unit, src, onward).start()


def chain_own(depth, z, hop, unit):
    for onward in (1, -1):

        @pl.when((z + onward >= 0) & (z + onward < depth))
        def _(onward=onward):
            hop(unit, z, onward).start()


def chain_sent(depth, z, hop, unit):
    for src in range(depth):

        @pl.when((src <= z) & (z < depth - 1))
        def _(src=src):
            hop(unit, src, 1).wait_send()

        @pl.when((src >= z) & (z > 0))
        def _(src=src):
            hop(unit, src, -1).wait_send()


def head_grads(k, values, codes, full, h, out):
    tokens, feats = k.shape
    half = feats // 2
    depth = full.shape[2]
    rates = (codes.astype(F32) + 1.0) / 16.0
    rates = jnp.transpose(jnp.broadcast_to(rates, (128, tokens)))
    rates = jnp.concatenate([rates] * (feats // 128), axis=1)
    target = (-rates * values.astype(F32)).astype(BF)
    for j in range(2):
        cols = pl.ds(j * half, half)
        gate = full[h, 0, :, :, :, :, cols].reshape(feats, half)
        up = full[h, 2, :, :, :, :, cols].reshape(feats, half)
        down = full[h, 1, pl.ds(j * (depth // 2), depth // 2)].reshape(half, feats)
        gate_pre = dot(k, gate)
        up_pre = dot(k, up)
        back = dot(target, down, ((1,), (1,)))
        sig = jax.nn.sigmoid(gate_pre)
        silu = gate_pre * sig
        hidden = (silu * up_pre).astype(BF)
        ggp = (back * up_pre * sig * (1.0 + gate_pre * (1.0 - sig))).astype(BF)
        gup = (back * silu).astype(BF)
        out[j, 0] = dot(k, ggp, ((0,), (0,))).astype(BF)
        out[j, 1] = dot(k, gup, ((0,), (0,))).astype(BF)
        gdown = dot(hidden, target, ((0,), (0,))).astype(BF)
        out[0, 2, cols, :] = gdown[:, :half]
        out[1, 2, cols, :] = gdown[:, half:]


def owner(depth, h):
    pos = h // WIDTH
    return jnp.where(pos % 2 == 0, pos // 2, depth - 1 - pos // 2)


def head_at(depth, h):
    return owner(depth, h) * WIDTH + h % WIDTH


def place_of(depth, z):
    return jnp.where(2 * z < depth, 2 * z, 2 * (depth - 1 - z) + 1)


def gather_kernel(
    depth, own, keys, values, codes, total, mine,
    full, kbuf, vbuf, obuf, got_c, paired, kept, got_x, summed, got_z,
    local, ksem, vsem, sr, sl, zr, xs, xr, ys, yr, cs, cr, gcs, gcr, gxs, gxr, gzs, gzr,
):
    heads = own.shape[0]
    z, x, s = place()
    y = lax.axis_index("groups")

    def load(h):
        slot = lax.rem(h, 2)
        return (
            pltpu.make_async_copy(keys.at[head_at(depth, h)], kbuf.at[slot], ksem.at[slot]),
            pltpu.make_async_copy(values.at[head_at(depth, h)], vbuf.at[slot], vsem.at[slot]),
        )

    for copy in load(0) + load(1):
        copy.start()
    pair = pl.ds(y, 2)
    keep = pltpu.make_async_copy(own.at[:, pair], full.at[:, pair, z, x, s], local)
    keep.start()
    greet(depth, z, x, s, ({"groups": 1 - y},))
    keep.wait()

    def hop(h, src, onward):
        block = full.at[h, pair, src, x, s]
        sems = sr if onward == 1 else sl
        return send(block, block, sems.at[h, src], zr.at[h, src], device(z + onward, x, s))

    def across(h, src):
        block = full.at[h, pair, src, x, s]
        return send(block, block, xs.at[h, src], xr.at[h, src], device(z, 1 - x, s))

    def over(h):
        block = full.at[h, 2 * y, :, :, s]
        return send(block, block, ys.at[h], yr.at[h], {"groups": 1 - y})

    def inside(h):
        block = full.at[h, :, :, :, s]
        return send(block, block, cs.at[h], cr.at[h], device(z, x, 1 - s))

    def first(h):
        chain_own(depth, z, hop, h)
        across(h, z).start()

    def hand(h):
        for src in range(depth):
            across(h, src).wait_recv()
        over(h).start()

    def spread(h):
        over(h).wait_recv()
        inside(h).start()

    def trade(h):
        return send(
            obuf.at[lax.rem(h, 2), 1 - s], got_c.at[h], gcs.at[h], gcr.at[h], device(z, x, 1 - s)
        )

    def deliver(zt):
        return send(paired.at[zt], got_x.at[zt], gxs.at[zt], gxr.at[zt], device(z, 1 - x, s))

    def along(zt):
        return send(summed.at[zt], got_z.at[z], gzs.at[zt], gzr.at[z], device(zt, x, s))

    def pair_up(h):
        zt = owner(depth, h)
        trade(h).wait_recv()
        slot = lax.rem(h, 2)
        ours = lax.rem(h, WIDTH) == x

        @pl.when(ours)
        def _():
            for m in range(3):
                kept[zt, m] = obuf[slot, s, m].astype(F32) + got_c[h, m].astype(F32)

        @pl.when(jnp.logical_not(ours))
        def _():
            for m in range(3):
                both = obuf[slot, s, m].astype(F32) + got_c[h, m].astype(F32)
                paired[zt, m] = both.astype(BF)
            deliver(zt).start()

    def join(h):
        zt = owner(depth, h)

        @pl.when(lax.rem(h, WIDTH) == WIDTH - 1)
        def _():
            deliver(zt).wait_recv()

            @pl.when(zt == z)
            def _():
                for m in range(3):
                    total[m] = kept[zt, m] + got_x[zt, m].astype(F32)

            @pl.when(zt != z)
            def _():
                for m in range(3):
                    summed[zt, m] = (kept[zt, m] + got_x[zt, m].astype(F32)).astype(BF)
                along(zt).start()

    def compute(h):
        slot = lax.rem(h, 2)
        inside(h).wait_recv()
        for copy in load(h):
            copy.wait()

        @pl.when(h >= 2)
        def _():
            trade(h - 2).wait_send()

        head_grads(kbuf[slot], vbuf[slot], codes[head_at(depth, h)], full, h, obuf.at[slot])
        trade(h).start()

        @pl.when(h + 2 < heads)
        def _():
            for copy in load(h + 2):
                copy.start()

    ahead = 2
    for h in range(ahead):
        first(h)

    def step(t, carry):
        def when(h, what):
            pl.when((h >= 0) & (h < heads))(lambda: what(h))

        when(t + ahead, first)
        when(t - depth, spread)
        when(t - depth + 1, hand)
        for k in range(depth - 1, 0, -1):
            when(t - k + 1, lambda h, k=k: chain(depth, z, hop, lambda u, i: across(u, i).start(), h, k))
        when(t - depth - 1, compute)
        when(t - depth - 2, pair_up)
        when(t - depth - 2 - late, join)
        return carry

    late = 2
    lax.fori_loop(0, heads + depth + 2 + late, step, 0)
    feats = mine.shape[1]
    for m in range(3):
        mine[m] = full[place_of(depth, z) * WIDTH + x, m].reshape(feats, feats)
    for k in range(1, depth):
        src = lax.rem(z + k, depth)
        send(
            summed.at[src], got_z.at[src], gzs.at[src], gzr.at[src], device(src, x, s)
        ).wait_recv()
        for m in range(3):
            total[m] += got_z[src, m].astype(F32)

    def last(h, carry):
        chain_sent(depth, z, hop, h)
        for src in range(depth):
            across(h, src).wait_send()
        over(h).wait_send()
        inside(h).wait_send()
        return carry

    lax.fori_loop(0, heads, last, 0)
    trade(heads - 2).wait_send()
    trade(heads - 1).wait_send()
    for zt in range(depth):
        deliver(zt).wait_send()
        pl.when(zt != z)(lambda zt=zt: along(zt).wait_send())


def learn(own, keys, values, codes, depth):
    heads, kinds, rows, cols = own.shape
    tokens, feats = keys.shape[1:]
    dma = pltpu.SemaphoreType.DMA
    vmem = pl.BlockSpec(memory_space=pltpu.VMEM)
    anywhere = pl.BlockSpec(memory_space=pl.ANY)
    piece = (kinds, feats, feats // 2)
    return pl.pallas_call(
        functools.partial(gather_kernel, depth),
        out_shape=(
            jax.ShapeDtypeStruct(piece, F32),
            jax.ShapeDtypeStruct((kinds, feats, feats), BF),
        ),
        in_specs=[vmem, anywhere, anywhere, vmem],
        out_specs=(vmem, vmem),
        scratch_shapes=[
            pltpu.VMEM((heads, kinds, depth, WIDTH, 2, rows, cols), BF),
            pltpu.VMEM((2, tokens, feats), BF),
            pltpu.VMEM((2, tokens, feats), BF),
            pltpu.VMEM((2, 2) + piece, BF),
            pltpu.VMEM((heads,) + piece, BF),
            pltpu.VMEM((depth,) + piece, BF),
            pltpu.VMEM((depth,) + piece, F32),
            pltpu.VMEM((depth,) + piece, BF),
            pltpu.VMEM((depth,) + piece, BF),
            pltpu.VMEM((depth,) + piece, BF),
            dma(()),
            dma((2,)),
            dma((2,)),
            *[dma((heads, depth))] * 5,
            *[dma((heads,))] * 6,
            *[dma((depth,))] * 4,
        ],
        compiler_params=pltpu.CompilerParams(
            collective_id=0, has_side_effects=True, vmem_limit_bytes=VMEM_LIMIT
        ),
        name="learn",
    )(own, keys, values, codes[:, None, :])


def apply_kernel(queries, weights, out):
    q = queries[0]
    half = weights.shape[-1]
    total = [None, None]
    for j in range(2):
        gate = dot(q, weights[0, j, 0])
        up = dot(q, weights[0, j, 1])
        hidden = (gate * jax.nn.sigmoid(gate) * up).astype(BF)
        for c in range(2):
            term = dot(hidden, weights[0, c, 2, pl.ds(j * half, half), :])
            total[c] = term if j == 0 else total[c] + term
    for c in range(2):
        out[0, :, pl.ds(c * half, half)] = total[c].astype(BF)


def apply_fast(queries, weights):
    heads, tokens, feats = queries.shape
    block = pl.BlockSpec((1, tokens, feats), lambda h: (h, 0, 0))
    return pl.pallas_call(
        apply_kernel,
        grid=(heads,),
        out_shape=jax.ShapeDtypeStruct(queries.shape, BF),
        in_specs=[
            block,
            pl.BlockSpec((1, 2, 3, feats, feats // 2), lambda h: (h, 0, 0, 0, 0)),
        ],
        out_specs=block,
        compiler_params=pltpu.CompilerParams(vmem_limit_bytes=VMEM_LIMIT),
        name="apply",
    )(queries, weights)


def renew_kernel(
    depth, total, weights, new, norm_out, norm_in, ns, nr, asr, asl, azr, axs, axr, acs, acr
):
    kinds, _, half = total.shape
    z, x, s = place()
    greet(depth, z, x, s)
    for m in range(kinds):
        part = total[m]
        norm_out[m] = jnp.broadcast_to(jnp.sum(part * part, keepdims=True), norm_out.shape[1:])
    norms = send(norm_out, norm_in, ns, nr, device(z, x, 1 - s))
    norms.start()
    norms.wait()

    def hop(m, src, onward):
        block = new.at[src, x, s, m]
        sems = asr if onward == 1 else asl
        return send(block, block, sems.at[m, src], azr.at[m, src], device(z + onward, x, s))

    def share_x(m, src):
        block = new.at[src, x, s, m]
        return send(block, block, axs.at[m, src], axr.at[m, src], device(z, 1 - x, s))

    def share_c(m, src):
        block = new.at[src, :, s, m]
        return send(block, block, acs.at[m, src], acr.at[m, src], device(z, x, 1 - s))

    def pass_on(m, src):
        share_x(m, src).wait_recv()
        share_c(m, src).start()

    for m in range(kinds):
        whole = weights[KIND[m]].astype(F32)
        weight_total = jnp.sum(whole * whole, keepdims=True)
        grad_total = norm_out[m, :1, :1] + norm_in[m, :1, :1]
        scale = STEP_SIZE * jnp.sqrt(weight_total + EPSILON) / jnp.sqrt(grad_total + EPSILON)
        own = weights[KIND[m], :, pl.ds(pl.multiple_of(s * half, half), half)].astype(F32)
        moved = own - scale * total[m]
        col_weight = jnp.sum(own * own, axis=0, keepdims=True)
        col_moved = jnp.sum(moved * moved, axis=0, keepdims=True)
        ratio = jnp.sqrt((col_weight + EPSILON) / (col_moved + EPSILON))
        new[z, x, s, m] = (moved * ratio).astype(BF)
        chain_own(depth, z, hop, m)
        share_x(m, z).start()
    for k in range(1, depth + 1):
        for m in range(kinds):
            if k < depth:
                chain(depth, z, hop, lambda u, i: share_x(u, i).start(), m, k)
            if k == 1:
                pass_on(m, z)
            else:
                pl.when(z - k + 1 >= 0)(lambda m=m, k=k: pass_on(m, z - k + 1))
                pl.when(z + k - 1 < depth)(lambda m=m, k=k: pass_on(m, z + k - 1))

    for m in range(kinds):
        chain_sent(depth, z, hop, m)
        for src in range(depth):
            share_x(m, src).wait_send()
            share_c(m, src).wait()


def renew(total, weights, depth):
    kinds, rows, half = total.shape
    dma = pltpu.SemaphoreType.DMA
    piece = (kinds, rows, half)
    new = pl.pallas_call(
        functools.partial(renew_kernel, depth),
        out_shape=jax.ShapeDtypeStruct((depth, WIDTH, 2) + piece, BF),
        in_specs=[pl.BlockSpec(memory_space=pltpu.VMEM)] * 2,
        out_specs=pl.BlockSpec(memory_space=pltpu.VMEM),
        scratch_shapes=[
            pltpu.VMEM((kinds, 8, 128), F32),
            pltpu.VMEM((kinds, 8, 128), F32),
            dma(()),
            dma(()),
            *[dma((kinds, depth))] * 7,
        ],
        compiler_params=pltpu.CompilerParams(
            collective_id=1, has_side_effects=True, vmem_limit_bytes=VMEM_LIMIT
        ),
        name="renew",
    )(total, weights)
    return new.reshape((depth * WIDTH, 2) + piece)


def on_device_heads(depth, queries, keys, values, lr_codes, fast_gate, fast_up, fast_down):
    own = jnp.stack([fast_gate, fast_down, fast_up], axis=1).astype(BF)
    rows = [p // 2 if p % 2 == 0 else depth - 1 - p // 2 for p in range(depth)]
    order = [r * WIDTH + x for r in rows for x in range(WIDTH)]
    own = jnp.stack([own[h] for h in order])
    total, mine = learn(own, keys, values, lr_codes, depth)
    new = renew(total, mine, depth)
    return apply_fast(queries, new)


def column_squares(matrix):
    return jnp.sum(matrix * matrix, axis=1)


def rescale(moved, col_weight, col_moved):
    return moved * jnp.sqrt((col_weight + EPSILON) / (col_moved + EPSILON))[:, None, :]


def step_scale(col_weight, grad_total):
    return (
        STEP_SIZE * jnp.sqrt(jnp.sum(col_weight, axis=1) + EPSILON) / jnp.sqrt(grad_total + EPSILON)
    )


def apply_rows(queries, gate_b, up_b, down_b):
    query_gate = jnp.einsum("htd,hdf->htf", queries, gate_b, preferred_element_type=jnp.float32)
    query_up = jnp.einsum("htd,hdf->htf", queries, up_b, preferred_element_type=jnp.float32)
    query_hidden = (jax.nn.silu(query_gate) * query_up).astype(jnp.bfloat16)
    return jnp.einsum(
        "htf,hfd->htd", query_hidden, down_b, preferred_element_type=jnp.float32
    ).astype(jnp.bfloat16)


def local_grads_rows(keys, target, gate_b, up_b, down_b):
    gate_pre = jnp.einsum("htd,hdf->htf", keys, gate_b, preferred_element_type=jnp.float32)
    up_pre = jnp.einsum("htd,hdf->htf", keys, up_b, preferred_element_type=jnp.float32)
    sigmoid_gate = jax.nn.sigmoid(gate_pre)
    hidden = (gate_pre * sigmoid_gate * up_pre).astype(jnp.bfloat16)
    back = jnp.einsum("htd,hfd->htf", target, down_b, preferred_element_type=jnp.float32)
    grad_gate_pre = (back * up_pre * sigmoid_gate * (1.0 + gate_pre * (1.0 - sigmoid_gate))).astype(
        jnp.bfloat16
    )
    grad_up_pre = (back * gate_pre * sigmoid_gate).astype(jnp.bfloat16)
    grad_gate = jnp.einsum("htd,htf->hdf", keys, grad_gate_pre, preferred_element_type=jnp.float32)
    grad_up = jnp.einsum("htd,htf->hdf", keys, grad_up_pre, preferred_element_type=jnp.float32)
    grad_down = jnp.einsum("htf,htd->hfd", hidden, target, preferred_element_type=jnp.float32)
    return (grad_gate, grad_up, grad_down)


def on_device_rows(queries, keys, values, lr_codes, fast_gate, fast_up, fast_down):
    token_rates = (lr_codes.astype(jnp.float32) + 1.0) / 16.0
    target = (-token_rates[:, :, None] * values.astype(jnp.float32)).astype(jnp.bfloat16)
    gate_b, up_b, down_b = (
        lax.all_gather(fast_gate.astype(jnp.bfloat16), ("seq", "sub"), axis=1, tiled=True),
        lax.all_gather(fast_up.astype(jnp.bfloat16), ("seq", "sub"), axis=1, tiled=True),
        lax.all_gather(fast_down.astype(jnp.bfloat16), ("seq", "sub"), axis=1, tiled=True),
    )
    grad_gate, grad_up, grad_down = local_grads_rows(keys, target, gate_b, up_b, down_b)
    owned = (
        lax.psum_scatter(grad_gate, ("seq", "sub"), scatter_dimension=1, tiled=True),
        lax.psum_scatter(grad_up, ("seq", "sub"), scatter_dimension=1, tiled=True),
        lax.psum_scatter(grad_down, ("seq", "sub"), scatter_dimension=1, tiled=True),
    )
    weights = (fast_gate, fast_up, fast_down)
    grad_local = jnp.stack(
        [
            jnp.sum(owned[0] * owned[0], axis=(1, 2)),
            jnp.sum(owned[1] * owned[1], axis=(1, 2)),
            jnp.sum(owned[2] * owned[2], axis=(1, 2)),
        ],
        axis=1,
    )
    col_gate, col_up, col_down, grad_totals = lax.psum(
        (column_squares(fast_gate), column_squares(fast_up), column_squares(fast_down), grad_local),
        ("seq", "sub"),
    )
    col_weights = (col_gate, col_up, col_down)
    moved_all = []
    for index in range(3):
        scale = step_scale(col_weights[index], grad_totals[:, index])
        moved_all.append(weights[index] - scale[:, None, None] * owned[index])
    moved_cols = lax.psum(
        (column_squares(moved_all[0]), column_squares(moved_all[1]), column_squares(moved_all[2])),
        ("seq", "sub"),
    )
    renewed = [
        rescale(moved_all[index], col_weights[index], moved_cols[index]).astype(jnp.bfloat16)
        for index in range(3)
    ]
    new_gate, new_up, new_down = (
        lax.all_gather(renewed[0], ("seq", "sub"), axis=1, tiled=True),
        lax.all_gather(renewed[1], ("seq", "sub"), axis=1, tiled=True),
        lax.all_gather(renewed[2], ("seq", "sub"), axis=1, tiled=True),
    )
    return apply_rows(queries, new_gate, new_up, new_down)


def solution(mesh):
    groups, seq, sub = (mesh.shape[axis] for axis in ("groups", "seq", "sub"))

    def on_device(*arrays):
        if groups == 2 and sub == 2 and seq % (2 * WIDTH) == 0 and arrays[4].shape[0] == seq:
            return on_device_heads(seq // WIDTH, *arrays)
        return on_device_rows(*arrays)

    return jax.shard_map(
        on_device,
        mesh=mesh,
        in_specs=(
            P("head", ("groups", "seq", "sub"), None),
            P("head", ("groups", "seq", "sub"), None),
            P("head", ("groups", "seq", "sub"), None),
            P("head", ("groups", "seq", "sub")),
            P("head", ("seq", "sub"), None),
            P("head", ("seq", "sub"), None),
            P("head", ("seq", "sub"), None),
        ),
        out_specs=P("head", ("groups", "seq", "sub"), None),
        check_vma=False,
    )
```

```python
import functools

import jax
import jax.numpy as jnp
from jax import lax
from jax.experimental import pallas as pl
from jax.experimental.pallas import tpu as pltpu
from jax.sharding import PartitionSpec as P

EPSILON = 1e-06
STEP_SIZE = 0.5
KIND = (0, 2, 1)
WIDTH = 2
VMEM_LIMIT = 60 * 1024 * 1024
BF = jnp.bfloat16
F32 = jnp.float32


def place():
    seq = lax.axis_index("seq")
    return lax.div(seq, WIDTH), lax.rem(seq, WIDTH), lax.axis_index("sub")


def device(z, x, s):
    return {"seq": z * WIDTH + x, "sub": s}


def greet(depth, z, x, s, others=()):
    barrier = pltpu.get_barrier_semaphore()
    partners = [device(lax.rem(z + k, depth), x, s) for k in range(1, depth)]
    partners += [device(z, 1 - x, s), device(z, x, 1 - s), *others]
    for partner in partners:
        pl.semaphore_signal(barrier, inc=1, device_id=partner, device_id_type=pl.DeviceIdType.MESH)
    pl.semaphore_wait(barrier, len(partners))


def send(src, dst, send_sem, recv_sem, target):
    return pltpu.make_async_remote_copy(
        src_ref=src,
        dst_ref=dst,
        send_sem=send_sem,
        recv_sem=recv_sem,
        device_id=target,
        device_id_type=pl.DeviceIdType.MESH,
    )


def dot(a, b, dims=((1,), (0,))):
    return lax.dot_general(a, b, (dims, ((), ())), preferred_element_type=F32)


def chain(depth, z, hop, started, unit, k):
    for back in (True, False):
        src = z - k if back else z + k
        onward = 1 if back else -1
        here = (src >= 0) if back else (src < depth)

        @pl.when(here)
        def _(src=src, onward=onward):
            hop(unit, src, -onward).wait_recv()
            started(unit, src)

            @pl.when((z + onward >= 0) & (z + onward < depth))
            def _():
                hop(unit, src, onward).start()


def chain_own(depth, z, hop, unit):
    for onward in (1, -1):

        @pl.when((z + onward >= 0) & (z + onward < depth))
        def _(onward=onward):
            hop(unit, z, onward).start()


def chain_sent(depth, z, hop, unit):
    for src in range(depth):

        @pl.when((src <= z) & (z < depth - 1))
        def _(src=src):
            hop(unit, src, 1).wait_send()

        @pl.when((src >= z) & (z > 0))
        def _(src=src):
            hop(unit, src, -1).wait_send()


def head_grads(k, values, codes, full, h, out):
    tokens, feats = k.shape
    half = feats // 2
    depth = full.shape[2]
    rates = (codes.astype(F32) + 1.0) / 16.0
    rates = jnp.transpose(jnp.broadcast_to(rates, (128, tokens)))
    rates = jnp.concatenate([rates] * (feats // 128), axis=1)
    target = (-rates * values.astype(F32)).astype(BF)
    for j in range(2):
        cols = pl.ds(j * half, half)
        gate = full[h, 0, :, :, :, :, cols].reshape(feats, half)
        up = full[h, 2, :, :, :, :, cols].reshape(feats, half)
        down = full[h, 1, pl.ds(j * (depth // 2), depth // 2)].reshape(half, feats)
        gate_pre = dot(k, gate)
        up_pre = dot(k, up)
        back = dot(target, down, ((1,), (1,)))
        sig = jax.nn.sigmoid(gate_pre)
        silu = gate_pre * sig
        hidden = (silu * up_pre).astype(BF)
        ggp = (back * up_pre * sig * (1.0 + gate_pre * (1.0 - sig))).astype(BF)
        gup = (back * silu).astype(BF)
        out[j, 0] = dot(k, ggp, ((0,), (0,))).astype(BF)
        out[j, 1] = dot(k, gup, ((0,), (0,))).astype(BF)
        gdown = dot(hidden, target, ((0,), (0,))).astype(BF)
        out[0, 2, cols, :] = gdown[:, :half]
        out[1, 2, cols, :] = gdown[:, half:]


def owner(depth, h):
    pos = h // WIDTH
    return jnp.where(pos % 2 == 0, pos // 2, depth - 1 - pos // 2)


def head_at(depth, h):
    return owner(depth, h) * WIDTH + h % WIDTH


def place_of(depth, z):
    return jnp.where(2 * z < depth, 2 * z, 2 * (depth - 1 - z) + 1)


def gather_kernel(
    depth, own, keys, values, codes, total, mine,
    full, kbuf, vbuf, obuf, got_c, paired, kept, got_x, summed, got_z,
    local, ksem, vsem, sr, sl, zr, xs, xr, ys, yr, cs, cr, gcs, gcr, gxs, gxr, gzs, gzr,
):
    heads = own.shape[0]
    z, x, s = place()
    y = lax.axis_index("groups")

    def load(h):
        slot = lax.rem(h, 2)
        return (
            pltpu.make_async_copy(keys.at[head_at(depth, h)], kbuf.at[slot], ksem.at[slot]),
            pltpu.make_async_copy(values.at[head_at(depth, h)], vbuf.at[slot], vsem.at[slot]),
        )

    for copy in load(0) + load(1):
        copy.start()
    pair = pl.ds(y, 2)
    keep = pltpu.make_async_copy(own.at[:, pair], full.at[:, pair, z, x, s], local)
    keep.start()
    greet(depth, z, x, s, ({"groups": 1 - y},))
    keep.wait()

    def hop(h, src, onward):
        block = full.at[h, pair, src, x, s]
        sems = sr if onward == 1 else sl
        return send(block, block, sems.at[h, src], zr.at[h, src], device(z + onward, x, s))

    def across(h, src):
        block = full.at[h, pair, src, x, s]
        return send(block, block, xs.at[h, src], xr.at[h, src], device(z, 1 - x, s))

    def over(h):
        block = full.at[h, 2 * y, :, :, s]
        return send(block, block, ys.at[h], yr.at[h], {"groups": 1 - y})

    def inside(h):
        block = full.at[h, :, :, :, s]
        return send(block, block, cs.at[h], cr.at[h], device(z, x, 1 - s))

    def first(h):
        chain_own(depth, z, hop, h)
        across(h, z).start()

    def hand(h):
        for src in range(depth):
            across(h, src).wait_recv()
        over(h).start()

    def spread(h):
        over(h).wait_recv()
        inside(h).start()

    def trade(h):
        return send(
            obuf.at[lax.rem(h, 2), 1 - s], got_c.at[h], gcs.at[h], gcr.at[h], device(z, x, 1 - s)
        )

    def deliver(zt, m):
        return send(
            paired.at[zt, m], got_x.at[zt, m], gxs.at[zt, m], gxr.at[zt, m], device(z, 1 - x, s)
        )

    def along(zt, m):
        return send(
            summed.at[zt, m], got_z.at[z, m], gzs.at[zt, m], gzr.at[z, m], device(zt, x, s)
        )

    def pair_up(h):
        zt = owner(depth, h)
        trade(h).wait_recv()
        slot = lax.rem(h, 2)
        ours = lax.rem(h, WIDTH) == x

        @pl.when(ours)
        def _():
            for m in range(3):
                kept[zt, m] = obuf[slot, s, m].astype(F32) + got_c[h, m].astype(F32)

        @pl.when(jnp.logical_not(ours))
        def _():
            for m in range(3):
                both = obuf[slot, s, m].astype(F32) + got_c[h, m].astype(F32)
                paired[zt, m] = both.astype(BF)
                deliver(zt, m).start()

    def join(h):
        zt = owner(depth, h)

        @pl.when(lax.rem(h, WIDTH) == WIDTH - 1)
        def _():
            @pl.when(zt == z)
            def _():
                for m in range(3):
                    deliver(zt, m).wait_recv()
                    total[m] = kept[zt, m] + got_x[zt, m].astype(F32)

            @pl.when(zt != z)
            def _():
                for m in range(3):
                    deliver(zt, m).wait_recv()
                    summed[zt, m] = (kept[zt, m] + got_x[zt, m].astype(F32)).astype(BF)
                    along(zt, m).start()

    def compute(h):
        slot = lax.rem(h, 2)
        inside(h).wait_recv()
        for copy in load(h):
            copy.wait()

        @pl.when(h >= 2)
        def _():
            trade(h - 2).wait_send()

        head_grads(kbuf[slot], vbuf[slot], codes[head_at(depth, h)], full, h, obuf.at[slot])
        trade(h).start()

        @pl.when(h + 2 < heads)
        def _():
            for copy in load(h + 2):
                copy.start()

    ahead = 2
    for h in range(ahead):
        first(h)

    def step(t, carry):
        def when(h, what):
            pl.when((h >= 0) & (h < heads))(lambda: what(h))

        when(t + ahead, first)
        when(t - depth, spread)
        when(t - depth + 1, hand)
        for k in range(depth - 1, 0, -1):
            when(t - k + 1, lambda h, k=k: chain(depth, z, hop, lambda u, i: across(u, i).start(), h, k))
        when(t - depth - 1, compute)
        when(t - depth - 2, pair_up)
        when(t - depth - 2 - late, join)
        return carry

    late = 2
    lax.fori_loop(0, heads + depth + 2 + late, step, 0)
    feats = mine.shape[1]
    for m in range(3):
        mine[m] = full[place_of(depth, z) * WIDTH + x, m].reshape(feats, feats)
    for k in range(1, depth):
        src = lax.rem(z + k, depth)
        for m in range(3):
            send(
                summed.at[src, m], got_z.at[src, m], gzs.at[src, m], gzr.at[src, m],
                device(src, x, s),
            ).wait_recv()
            total[m] += got_z[src, m].astype(F32)

    def last(h, carry):
        chain_sent(depth, z, hop, h)
        for src in range(depth):
            across(h, src).wait_send()
        over(h).wait_send()
        inside(h).wait_send()
        return carry

    lax.fori_loop(0, heads, last, 0)
    trade(heads - 2).wait_send()
    trade(heads - 1).wait_send()
    for zt in range(depth):
        for m in range(3):
            deliver(zt, m).wait_send()
            pl.when(zt != z)(lambda zt=zt, m=m: along(zt, m).wait_send())


def learn(own, keys, values, codes, depth):
    heads, kinds, rows, cols = own.shape
    tokens, feats = keys.shape[1:]
    dma = pltpu.SemaphoreType.DMA
    vmem = pl.BlockSpec(memory_space=pltpu.VMEM)
    anywhere = pl.BlockSpec(memory_space=pl.ANY)
    piece = (kinds, feats, feats // 2)
    return pl.pallas_call(
        functools.partial(gather_kernel, depth),
        out_shape=(
            jax.ShapeDtypeStruct(piece, F32),
            jax.ShapeDtypeStruct((kinds, feats, feats), BF),
        ),
        in_specs=[vmem, anywhere, anywhere, vmem],
        out_specs=(vmem, vmem),
        scratch_shapes=[
            pltpu.VMEM((heads, kinds, depth, WIDTH, 2, rows, cols), BF),
            pltpu.VMEM((2, tokens, feats), BF),
            pltpu.VMEM((2, tokens, feats), BF),
            pltpu.VMEM((2, 2) + piece, BF),
            pltpu.VMEM((heads,) + piece, BF),
            pltpu.VMEM((depth,) + piece, BF),
            pltpu.VMEM((depth,) + piece, F32),
            pltpu.VMEM((depth,) + piece, BF),
            pltpu.VMEM((depth,) + piece, BF),
            pltpu.VMEM((depth,) + piece, BF),
            dma(()),
            dma((2,)),
            dma((2,)),
            *[dma((heads, depth))] * 5,
            *[dma((heads,))] * 6,
            *[dma((depth, kinds))] * 4,
        ],
        compiler_params=pltpu.CompilerParams(
            collective_id=0, has_side_effects=True, vmem_limit_bytes=VMEM_LIMIT
        ),
        name="learn",
    )(own, keys, values, codes[:, None, :])


def apply_kernel(queries, weights, out):
    q = queries[0]
    half = weights.shape[-1]
    total = [None, None]
    for j in range(2):
        gate = dot(q, weights[0, j, 0])
        up = dot(q, weights[0, j, 1])
        hidden = (gate * jax.nn.sigmoid(gate) * up).astype(BF)
        for c in range(2):
            term = dot(hidden, weights[0, c, 2, pl.ds(j * half, half), :])
            total[c] = term if j == 0 else total[c] + term
    for c in range(2):
        out[0, :, pl.ds(c * half, half)] = total[c].astype(BF)


def apply_fast(queries, weights):
    heads, tokens, feats = queries.shape
    block = pl.BlockSpec((1, tokens, feats), lambda h: (h, 0, 0))
    return pl.pallas_call(
        apply_kernel,
        grid=(heads,),
        out_shape=jax.ShapeDtypeStruct(queries.shape, BF),
        in_specs=[
            block,
            pl.BlockSpec((1, 2, 3, feats, feats // 2), lambda h: (h, 0, 0, 0, 0)),
        ],
        out_specs=block,
        compiler_params=pltpu.CompilerParams(vmem_limit_bytes=VMEM_LIMIT),
        name="apply",
    )(queries, weights)


def renew_kernel(
    depth, total, weights, new, norm_out, norm_in, ns, nr, asr, asl, azr, axs, axr, acs, acr
):
    kinds, rows, half = total.shape
    z, x, s = place()
    greet(depth, z, x, s)
    for m in range(kinds):
        part = total[m]
        norm_out[m] = jnp.broadcast_to(jnp.sum(part * part, keepdims=True), norm_out.shape[1:])
    norms = send(norm_out, norm_in, ns, nr, device(z, x, 1 - s))
    norms.start()
    norms.wait()

    part = rows // 2
    units = ((2, part, rows - part, True), (2, 0, part, False), (0, 0, rows, False), (1, 0, rows, False))

    def block(u, src, col):
        m, begin, count, _ = units[u]
        return new.at[src, col, s, m, pl.ds(begin, count)]

    def hop(unit, src, onward):
        u, c = unit
        piece = block(u, src, 1 - x if c else x)
        sems = asr if onward == 1 else asl
        return send(piece, piece, sems.at[u, c, src], azr.at[u, c, src], device(z + onward, x, s))

    def share_x(u, src):
        piece = block(u, src, x)
        return send(piece, piece, axs.at[u, src], axr.at[u, src], device(z, 1 - x, s))

    def share_c(u, src):
        piece = block(u, src, slice(None))
        return send(piece, piece, acs.at[u, src], acr.at[u, src], device(z, x, 1 - s))

    def pass_on(u, src):
        if not units[u][3]:
            share_x(u, src).wait_recv()
        share_c(u, src).start()

    def arrived(unit, src):
        if not units[unit[0]][3]:
            share_x(unit[0], src).start()

    for m in (2, 0, 1):
        whole = weights[KIND[m]].astype(F32)
        weight_total = jnp.sum(whole * whole, keepdims=True)
        grad_total = norm_out[m, :1, :1] + norm_in[m, :1, :1]
        scale = STEP_SIZE * jnp.sqrt(weight_total + EPSILON) / jnp.sqrt(grad_total + EPSILON)
        own = weights[KIND[m], :, pl.ds(pl.multiple_of(s * half, half), half)].astype(F32)
        moved = own - scale * total[m]
        col_weight = jnp.sum(own * own, axis=0, keepdims=True)
        col_moved = jnp.sum(moved * moved, axis=0, keepdims=True)
        ratio = jnp.sqrt((col_weight + EPSILON) / (col_moved + EPSILON))
        new[z, x, s, m] = (moved * ratio).astype(BF)
        for u in range(len(units)):
            if units[u][0] == m:
                share_x(u, z).start()
                chain_own(depth, z, hop, (u, 0))
    share_x(0, z).wait_recv()
    chain_own(depth, z, hop, (0, 1))
    for k in range(1, depth + 1):
        for u in (1, 2, 3, 0):
            if k < depth:
                for c in range(2 if units[u][3] else 1):
                    chain(depth, z, hop, arrived, (u, c), k)
            if k == 1:
                pass_on(u, z)
            else:
                pl.when(z - k + 1 >= 0)(lambda u=u, k=k: pass_on(u, z - k + 1))
                pl.when(z + k - 1 < depth)(lambda u=u, k=k: pass_on(u, z + k - 1))

    for u in range(len(units)):
        for c in range(2 if units[u][3] else 1):
            chain_sent(depth, z, hop, (u, c))
        if units[u][3]:
            share_x(u, z).wait_send()
        for src in range(depth):
            if not units[u][3]:
                share_x(u, src).wait_send()
            share_c(u, src).wait()


def renew(total, weights, depth):
    kinds, rows, half = total.shape
    dma = pltpu.SemaphoreType.DMA
    piece = (kinds, rows, half)
    new = pl.pallas_call(
        functools.partial(renew_kernel, depth),
        out_shape=jax.ShapeDtypeStruct((depth, WIDTH, 2) + piece, BF),
        in_specs=[pl.BlockSpec(memory_space=pltpu.VMEM)] * 2,
        out_specs=pl.BlockSpec(memory_space=pltpu.VMEM),
        scratch_shapes=[
            pltpu.VMEM((kinds, 8, 128), F32),
            pltpu.VMEM((kinds, 8, 128), F32),
            dma(()),
            dma(()),
            *[dma((4, 2, depth))] * 3,
            *[dma((4, depth))] * 4,
        ],
        compiler_params=pltpu.CompilerParams(
            collective_id=1, has_side_effects=True, vmem_limit_bytes=VMEM_LIMIT
        ),
        name="renew",
    )(total, weights)
    return new.reshape((depth * WIDTH, 2) + piece)


def on_device_heads(depth, queries, keys, values, lr_codes, fast_gate, fast_up, fast_down):
    own = jnp.stack([fast_gate, fast_down, fast_up], axis=1).astype(BF)
    rows = [p // 2 if p % 2 == 0 else depth - 1 - p // 2 for p in range(depth)]
    order = [r * WIDTH + x for r in rows for x in range(WIDTH)]
    own = jnp.stack([own[h] for h in order])
    total, mine = learn(own, keys, values, lr_codes, depth)
    new = renew(total, mine, depth)
    return apply_fast(queries, new)


def column_squares(matrix):
    return jnp.sum(matrix * matrix, axis=1)


def rescale(moved, col_weight, col_moved):
    return moved * jnp.sqrt((col_weight + EPSILON) / (col_moved + EPSILON))[:, None, :]


def step_scale(col_weight, grad_total):
    return (
        STEP_SIZE * jnp.sqrt(jnp.sum(col_weight, axis=1) + EPSILON) / jnp.sqrt(grad_total + EPSILON)
    )


def apply_rows(queries, gate_b, up_b, down_b):
    query_gate = jnp.einsum("htd,hdf->htf", queries, gate_b, preferred_element_type=jnp.float32)
    query_up = jnp.einsum("htd,hdf->htf", queries, up_b, preferred_element_type=jnp.float32)
    query_hidden = (jax.nn.silu(query_gate) * query_up).astype(jnp.bfloat16)
    return jnp.einsum(
        "htf,hfd->htd", query_hidden, down_b, preferred_element_type=jnp.float32
    ).astype(jnp.bfloat16)


def local_grads_rows(keys, target, gate_b, up_b, down_b):
    gate_pre = jnp.einsum("htd,hdf->htf", keys, gate_b, preferred_element_type=jnp.float32)
    up_pre = jnp.einsum("htd,hdf->htf", keys, up_b, preferred_element_type=jnp.float32)
    sigmoid_gate = jax.nn.sigmoid(gate_pre)
    hidden = (gate_pre * sigmoid_gate * up_pre).astype(jnp.bfloat16)
    back = jnp.einsum("htd,hfd->htf", target, down_b, preferred_element_type=jnp.float32)
    grad_gate_pre = (back * up_pre * sigmoid_gate * (1.0 + gate_pre * (1.0 - sigmoid_gate))).astype(
        jnp.bfloat16
    )
    grad_up_pre = (back * gate_pre * sigmoid_gate).astype(jnp.bfloat16)
    grad_gate = jnp.einsum("htd,htf->hdf", keys, grad_gate_pre, preferred_element_type=jnp.float32)
    grad_up = jnp.einsum("htd,htf->hdf", keys, grad_up_pre, preferred_element_type=jnp.float32)
    grad_down = jnp.einsum("htf,htd->hfd", hidden, target, preferred_element_type=jnp.float32)
    return (grad_gate, grad_up, grad_down)


def on_device_rows(queries, keys, values, lr_codes, fast_gate, fast_up, fast_down):
    token_rates = (lr_codes.astype(jnp.float32) + 1.0) / 16.0
    target = (-token_rates[:, :, None] * values.astype(jnp.float32)).astype(jnp.bfloat16)
    gate_b, up_b, down_b = (
        lax.all_gather(fast_gate.astype(jnp.bfloat16), ("seq", "sub"), axis=1, tiled=True),
        lax.all_gather(fast_up.astype(jnp.bfloat16), ("seq", "sub"), axis=1, tiled=True),
        lax.all_gather(fast_down.astype(jnp.bfloat16), ("seq", "sub"), axis=1, tiled=True),
    )
    grad_gate, grad_up, grad_down = local_grads_rows(keys, target, gate_b, up_b, down_b)
    owned = (
        lax.psum_scatter(grad_gate, ("seq", "sub"), scatter_dimension=1, tiled=True),
        lax.psum_scatter(grad_up, ("seq", "sub"), scatter_dimension=1, tiled=True),
        lax.psum_scatter(grad_down, ("seq", "sub"), scatter_dimension=1, tiled=True),
    )
    weights = (fast_gate, fast_up, fast_down)
    grad_local = jnp.stack(
        [
            jnp.sum(owned[0] * owned[0], axis=(1, 2)),
            jnp.sum(owned[1] * owned[1], axis=(1, 2)),
            jnp.sum(owned[2] * owned[2], axis=(1, 2)),
        ],
        axis=1,
    )
    col_gate, col_up, col_down, grad_totals = lax.psum(
        (column_squares(fast_gate), column_squares(fast_up), column_squares(fast_down), grad_local),
        ("seq", "sub"),
    )
    col_weights = (col_gate, col_up, col_down)
    moved_all = []
    for index in range(3):
        scale = step_scale(col_weights[index], grad_totals[:, index])
        moved_all.append(weights[index] - scale[:, None, None] * owned[index])
    moved_cols = lax.psum(
        (column_squares(moved_all[0]), column_squares(moved_all[1]), column_squares(moved_all[2])),
        ("seq", "sub"),
    )
    renewed = [
        rescale(moved_all[index], col_weights[index], moved_cols[index]).astype(jnp.bfloat16)
        for index in range(3)
    ]
    new_gate, new_up, new_down = (
        lax.all_gather(renewed[0], ("seq", "sub"), axis=1, tiled=True),
        lax.all_gather(renewed[1], ("seq", "sub"), axis=1, tiled=True),
        lax.all_gather(renewed[2], ("seq", "sub"), axis=1, tiled=True),
    )
    return apply_rows(queries, new_gate, new_up, new_down)


def solution(mesh):
    groups, seq, sub = (mesh.shape[axis] for axis in ("groups", "seq", "sub"))

    def on_device(*arrays):
        if groups == 2 and sub == 2 and seq % (2 * WIDTH) == 0 and arrays[4].shape[0] == seq:
            return on_device_heads(seq // WIDTH, *arrays)
        return on_device_rows(*arrays)

    return jax.shard_map(
        on_device,
        mesh=mesh,
        in_specs=(
            P("head", ("groups", "seq", "sub"), None),
            P("head", ("groups", "seq", "sub"), None),
            P("head", ("groups", "seq", "sub"), None),
            P("head", ("groups", "seq", "sub")),
            P("head", ("seq", "sub"), None),
            P("head", ("seq", "sub"), None),
            P("head", ("seq", "sub"), None),
        ),
        out_specs=P("head", ("groups", "seq", "sub"), None),
        check_vma=False,
    )
```

```python
import functools

import jax
import jax.numpy as jnp
from jax import lax
from jax.experimental import pallas as pl
from jax.experimental.pallas import tpu as pltpu
from jax.sharding import PartitionSpec as P

EPSILON = 1e-06
STEP_SIZE = 0.5
KIND = (0, 2, 1)
WIDTH = 2
VMEM_LIMIT = 60 * 1024 * 1024
BF = jnp.bfloat16
F32 = jnp.float32


def place():
    seq = lax.axis_index("seq")
    return lax.div(seq, WIDTH), lax.rem(seq, WIDTH), lax.axis_index("sub")


def device(z, x, s):
    return {"seq": z * WIDTH + x, "sub": s}


def greet(depth, z, x, s, others=()):
    barrier = pltpu.get_barrier_semaphore()
    partners = [device(lax.rem(z + k, depth), x, s) for k in range(1, depth)]
    partners += [device(z, 1 - x, s), device(z, x, 1 - s), *others]
    for partner in partners:
        pl.semaphore_signal(barrier, inc=1, device_id=partner, device_id_type=pl.DeviceIdType.MESH)
    pl.semaphore_wait(barrier, len(partners))


def send(src, dst, send_sem, recv_sem, target):
    return pltpu.make_async_remote_copy(
        src_ref=src,
        dst_ref=dst,
        send_sem=send_sem,
        recv_sem=recv_sem,
        device_id=target,
        device_id_type=pl.DeviceIdType.MESH,
    )


def dot(a, b, dims=((1,), (0,))):
    return lax.dot_general(a, b, (dims, ((), ())), preferred_element_type=F32)


def chain(depth, z, hop, started, unit, k):
    for back in (True, False):
        src = z - k if back else z + k
        onward = 1 if back else -1
        here = (src >= 0) if back else (src < depth)

        @pl.when(here)
        def _(src=src, onward=onward):
            hop(unit, src, -onward).wait_recv()
            started(unit, src)

            @pl.when((z + onward >= 0) & (z + onward < depth))
            def _():
                hop(unit, src, onward).start()


def chain_own(depth, z, hop, unit):
    for onward in (1, -1):

        @pl.when((z + onward >= 0) & (z + onward < depth))
        def _(onward=onward):
            hop(unit, z, onward).start()


def chain_sent(depth, z, hop, unit):
    for src in range(depth):

        @pl.when((src <= z) & (z < depth - 1))
        def _(src=src):
            hop(unit, src, 1).wait_send()

        @pl.when((src >= z) & (z > 0))
        def _(src=src):
            hop(unit, src, -1).wait_send()


def head_grads(k, values, codes, full, h, out):
    tokens, feats = k.shape
    half = feats // 2
    depth = full.shape[2]
    rates = (codes.astype(F32) + 1.0) / 16.0
    rates = jnp.transpose(jnp.broadcast_to(rates, (128, tokens)))
    rates = jnp.concatenate([rates] * (feats // 128), axis=1)
    target = (-rates * values.astype(F32)).astype(BF)
    for j in range(2):
        cols = pl.ds(j * half, half)
        gate = full[h, 0, :, :, :, :, cols].reshape(feats, half)
        up = full[h, 2, :, :, :, :, cols].reshape(feats, half)
        down = full[h, 1, pl.ds(j * (depth // 2), depth // 2)].reshape(half, feats)
        gate_pre = dot(k, gate)
        up_pre = dot(k, up)
        back = dot(target, down, ((1,), (1,)))
        sig = jax.nn.sigmoid(gate_pre)
        silu = gate_pre * sig
        hidden = (silu * up_pre).astype(BF)
        ggp = (back * up_pre * sig * (1.0 + gate_pre * (1.0 - sig))).astype(BF)
        gup = (back * silu).astype(BF)
        out[j, 0] = dot(k, ggp, ((0,), (0,))).astype(BF)
        out[j, 1] = dot(k, gup, ((0,), (0,))).astype(BF)
        gdown = dot(hidden, target, ((0,), (0,))).astype(BF)
        out[0, 2, cols, :] = gdown[:, :half]
        out[1, 2, cols, :] = gdown[:, half:]


def owner(depth, h):
    pos = h // WIDTH
    return jnp.where(pos % 2 == 0, pos // 2, depth - 1 - pos // 2)


def head_at(depth, h):
    return owner(depth, h) * WIDTH + h % WIDTH


def place_of(depth, z):
    return jnp.where(2 * z < depth, 2 * z, 2 * (depth - 1 - z) + 1)


def gather_kernel(
    depth, own, keys, values, codes, total, mine,
    full, kbuf, vbuf, obuf, got_c, paired, kept, got_x, summed, got_z,
    local, ksem, vsem, sr, sl, zr, xs, xr, ys, yr, cs, cr, gcs, gcr, gxs, gxr, gzs, gzr,
):
    heads = own.shape[0]
    z, x, s = place()
    y = lax.axis_index("groups")

    def load(h):
        slot = lax.rem(h, 2)
        return (
            pltpu.make_async_copy(keys.at[head_at(depth, h)], kbuf.at[slot], ksem.at[slot]),
            pltpu.make_async_copy(values.at[head_at(depth, h)], vbuf.at[slot], vsem.at[slot]),
        )

    for copy in load(0) + load(1):
        copy.start()
    pair = pl.ds(y, 2)
    keep = pltpu.make_async_copy(own.at[:, pair], full.at[:, pair, z, x, s], local)
    keep.start()
    greet(depth, z, x, s, ({"groups": 1 - y},))
    keep.wait()

    def hop(h, src, onward):
        block = full.at[h, pair, src, x, s]
        sems = sr if onward == 1 else sl
        return send(block, block, sems.at[h, src], zr.at[h, src], device(z + onward, x, s))

    def across(h, src):
        block = full.at[h, pair, src, x, s]
        return send(block, block, xs.at[h, src], xr.at[h, src], device(z, 1 - x, s))

    def over(h):
        block = full.at[h, 2 * y, :, :, s]
        return send(block, block, ys.at[h], yr.at[h], {"groups": 1 - y})

    def inside(h):
        block = full.at[h, :, :, :, s]
        return send(block, block, cs.at[h], cr.at[h], device(z, x, 1 - s))

    def first(h):
        chain_own(depth, z, hop, h)
        across(h, z).start()

    def hand(h):
        for src in range(depth):
            across(h, src).wait_recv()
        over(h).start()

    def spread(h):
        over(h).wait_recv()
        inside(h).start()

    def trade(h):
        return send(
            obuf.at[lax.rem(h, 2), 1 - s], got_c.at[h], gcs.at[h], gcr.at[h], device(z, x, 1 - s)
        )

    def deliver(zt, m):
        return send(
            paired.at[zt, m], got_x.at[zt, m], gxs.at[zt, m], gxr.at[zt, m], device(z, 1 - x, s)
        )

    def along(zt, m):
        return send(
            summed.at[zt, m], got_z.at[z, m], gzs.at[zt, m], gzr.at[z, m], device(zt, x, s)
        )

    def pair_up(h):
        zt = owner(depth, h)
        trade(h).wait_recv()
        slot = lax.rem(h, 2)
        ours = lax.rem(h, WIDTH) == x

        @pl.when(ours)
        def _():
            for m in range(3):
                kept[zt, m] = obuf[slot, s, m].astype(F32) + got_c[h, m].astype(F32)

        @pl.when(jnp.logical_not(ours))
        def _():
            for m in range(3):
                both = obuf[slot, s, m].astype(F32) + got_c[h, m].astype(F32)
                paired[zt, m] = both.astype(BF)
                deliver(zt, m).start()

    def join(h):
        zt = owner(depth, h)

        @pl.when(lax.rem(h, WIDTH) == WIDTH - 1)
        def _():
            @pl.when(zt == z)
            def _():
                for m in range(3):
                    deliver(zt, m).wait_recv()
                    total[m] = kept[zt, m] + got_x[zt, m].astype(F32)

            @pl.when(zt != z)
            def _():
                for m in range(3):
                    deliver(zt, m).wait_recv()
                    summed[zt, m] = (kept[zt, m] + got_x[zt, m].astype(F32)).astype(BF)
                    along(zt, m).start()

    def compute(h):
        slot = lax.rem(h, 2)
        inside(h).wait_recv()
        for copy in load(h):
            copy.wait()

        @pl.when(h >= 2)
        def _():
            trade(h - 2).wait_send()

        head_grads(kbuf[slot], vbuf[slot], codes[head_at(depth, h)], full, h, obuf.at[slot])
        trade(h).start()

        @pl.when(h + 2 < heads)
        def _():
            for copy in load(h + 2):
                copy.start()

    ahead = 2
    for h in range(ahead):
        first(h)

    def step(t, carry):
        def when(h, what):
            pl.when((h >= 0) & (h < heads))(lambda: what(h))

        when(t + ahead, first)
        when(t - depth, spread)
        when(t - depth + 1, hand)
        for k in range(depth - 1, 0, -1):
            when(t - k + 1, lambda h, k=k: chain(depth, z, hop, lambda u, i: across(u, i).start(), h, k))
        when(t - depth - 2, pair_up)
        when(t - depth - 1, compute)
        when(t - depth - 2 - late, join)
        return carry

    late = 2
    lax.fori_loop(0, heads + depth + 2 + late, step, 0)
    feats = mine.shape[1]
    for m in range(3):
        mine[m] = full[place_of(depth, z) * WIDTH + x, m].reshape(feats, feats)
    for k in range(1, depth):
        src = lax.rem(z + k, depth)
        for m in range(3):
            send(
                summed.at[src, m], got_z.at[src, m], gzs.at[src, m], gzr.at[src, m],
                device(src, x, s),
            ).wait_recv()
            total[m] += got_z[src, m].astype(F32)

    def last(h, carry):
        chain_sent(depth, z, hop, h)
        for src in range(depth):
            across(h, src).wait_send()
        over(h).wait_send()
        inside(h).wait_send()
        return carry

    lax.fori_loop(0, heads, last, 0)
    trade(heads - 2).wait_send()
    trade(heads - 1).wait_send()
    for zt in range(depth):
        for m in range(3):
            deliver(zt, m).wait_send()
            pl.when(zt != z)(lambda zt=zt, m=m: along(zt, m).wait_send())


def learn(own, keys, values, codes, depth):
    heads, kinds, rows, cols = own.shape
    tokens, feats = keys.shape[1:]
    dma = pltpu.SemaphoreType.DMA
    vmem = pl.BlockSpec(memory_space=pltpu.VMEM)
    anywhere = pl.BlockSpec(memory_space=pl.ANY)
    piece = (kinds, feats, feats // 2)
    return pl.pallas_call(
        functools.partial(gather_kernel, depth),
        out_shape=(
            jax.ShapeDtypeStruct(piece, F32),
            jax.ShapeDtypeStruct((kinds, feats, feats), BF),
        ),
        in_specs=[vmem, anywhere, anywhere, vmem],
        out_specs=(vmem, vmem),
        scratch_shapes=[
            pltpu.VMEM((heads, kinds, depth, WIDTH, 2, rows, cols), BF),
            pltpu.VMEM((2, tokens, feats), BF),
            pltpu.VMEM((2, tokens, feats), BF),
            pltpu.VMEM((2, 2) + piece, BF),
            pltpu.VMEM((heads,) + piece, BF),
            pltpu.VMEM((depth,) + piece, BF),
            pltpu.VMEM((depth,) + piece, F32),
            pltpu.VMEM((depth,) + piece, BF),
            pltpu.VMEM((depth,) + piece, BF),
            pltpu.VMEM((depth,) + piece, BF),
            dma(()),
            dma((2,)),
            dma((2,)),
            *[dma((heads, depth))] * 5,
            *[dma((heads,))] * 6,
            *[dma((depth, kinds))] * 4,
        ],
        compiler_params=pltpu.CompilerParams(
            collective_id=0, has_side_effects=True, vmem_limit_bytes=VMEM_LIMIT
        ),
        name="learn",
    )(own, keys, values, codes[:, None, :])


def apply_kernel(queries, weights, out):
    q = queries[0]
    half = weights.shape[-1]
    total = [None, None]
    for j in range(2):
        gate = dot(q, weights[0, j, 0])
        up = dot(q, weights[0, j, 1])
        hidden = (gate * jax.nn.sigmoid(gate) * up).astype(BF)
        for c in range(2):
            term = dot(hidden, weights[0, c, 2, pl.ds(j * half, half), :])
            total[c] = term if j == 0 else total[c] + term
    for c in range(2):
        out[0, :, pl.ds(c * half, half)] = total[c].astype(BF)


def apply_fast(queries, weights):
    heads, tokens, feats = queries.shape
    block = pl.BlockSpec((1, tokens, feats), lambda h: (h, 0, 0))
    return pl.pallas_call(
        apply_kernel,
        grid=(heads,),
        out_shape=jax.ShapeDtypeStruct(queries.shape, BF),
        in_specs=[
            block,
            pl.BlockSpec((1, 2, 3, feats, feats // 2), lambda h: (h, 0, 0, 0, 0)),
        ],
        out_specs=block,
        compiler_params=pltpu.CompilerParams(vmem_limit_bytes=VMEM_LIMIT),
        name="apply",
    )(queries, weights)


def renew_kernel(
    depth, total, weights, new, norm_out, norm_in, ns, nr, asr, asl, azr, axs, axr, acs, acr
):
    kinds, rows, half = total.shape
    z, x, s = place()
    greet(depth, z, x, s)
    for m in range(kinds):
        part = total[m]
        norm_out[m] = jnp.broadcast_to(jnp.sum(part * part, keepdims=True), norm_out.shape[1:])
    norms = send(norm_out, norm_in, ns, nr, device(z, x, 1 - s))
    norms.start()
    norms.wait()

    part = rows // 2
    units = ((2, part, rows - part, True), (2, 0, part, False), (0, 0, rows, False), (1, 0, rows, False))

    def block(u, src, col):
        m, begin, count, _ = units[u]
        return new.at[src, col, s, m, pl.ds(begin, count)]

    def hop(unit, src, onward):
        u, c = unit
        piece = block(u, src, 1 - x if c else x)
        sems = asr if onward == 1 else asl
        return send(piece, piece, sems.at[u, c, src], azr.at[u, c, src], device(z + onward, x, s))

    def share_x(u, src):
        piece = block(u, src, x)
        return send(piece, piece, axs.at[u, src], axr.at[u, src], device(z, 1 - x, s))

    def share_c(u, src):
        piece = block(u, src, slice(None))
        return send(piece, piece, acs.at[u, src], acr.at[u, src], device(z, x, 1 - s))

    def pass_on(u, src):
        if not units[u][3]:
            share_x(u, src).wait_recv()
        share_c(u, src).start()

    def arrived(unit, src):
        if not units[unit[0]][3]:
            share_x(unit[0], src).start()

    for m in (2, 0, 1):
        whole = weights[KIND[m]].astype(F32)
        weight_total = jnp.sum(whole * whole, keepdims=True)
        grad_total = norm_out[m, :1, :1] + norm_in[m, :1, :1]
        scale = STEP_SIZE * jnp.sqrt(weight_total + EPSILON) / jnp.sqrt(grad_total + EPSILON)
        own = weights[KIND[m], :, pl.ds(pl.multiple_of(s * half, half), half)].astype(F32)
        moved = own - scale * total[m]
        col_weight = jnp.sum(own * own, axis=0, keepdims=True)
        col_moved = jnp.sum(moved * moved, axis=0, keepdims=True)
        ratio = jnp.sqrt((col_weight + EPSILON) / (col_moved + EPSILON))
        new[z, x, s, m] = (moved * ratio).astype(BF)
        for u in range(len(units)):
            if units[u][0] == m:
                share_x(u, z).start()
                chain_own(depth, z, hop, (u, 0))
    share_x(0, z).wait_recv()
    chain_own(depth, z, hop, (0, 1))
    for k in range(1, depth + 1):
        for u in (1, 2, 3, 0):
            if k < depth:
                for c in range(2 if units[u][3] else 1):
                    chain(depth, z, hop, arrived, (u, c), k)
            if k == 1:
                pass_on(u, z)
            else:
                pl.when(z - k + 1 >= 0)(lambda u=u, k=k: pass_on(u, z - k + 1))
                pl.when(z + k - 1 < depth)(lambda u=u, k=k: pass_on(u, z + k - 1))

    for u in range(len(units)):
        for c in range(2 if units[u][3] else 1):
            chain_sent(depth, z, hop, (u, c))
        if units[u][3]:
            share_x(u, z).wait_send()
        for src in range(depth):
            if not units[u][3]:
                share_x(u, src).wait_send()
            share_c(u, src).wait()


def renew(total, weights, depth):
    kinds, rows, half = total.shape
    dma = pltpu.SemaphoreType.DMA
    piece = (kinds, rows, half)
    new = pl.pallas_call(
        functools.partial(renew_kernel, depth),
        out_shape=jax.ShapeDtypeStruct((depth, WIDTH, 2) + piece, BF),
        in_specs=[pl.BlockSpec(memory_space=pltpu.VMEM)] * 2,
        out_specs=pl.BlockSpec(memory_space=pltpu.VMEM),
        scratch_shapes=[
            pltpu.VMEM((kinds, 8, 128), F32),
            pltpu.VMEM((kinds, 8, 128), F32),
            dma(()),
            dma(()),
            *[dma((4, 2, depth))] * 3,
            *[dma((4, depth))] * 4,
        ],
        compiler_params=pltpu.CompilerParams(
            collective_id=1, has_side_effects=True, vmem_limit_bytes=VMEM_LIMIT
        ),
        name="renew",
    )(total, weights)
    return new.reshape((depth * WIDTH, 2) + piece)


def on_device_heads(depth, queries, keys, values, lr_codes, fast_gate, fast_up, fast_down):
    own = jnp.stack([fast_gate, fast_down, fast_up], axis=1).astype(BF)
    rows = [p // 2 if p % 2 == 0 else depth - 1 - p // 2 for p in range(depth)]
    order = [r * WIDTH + x for r in rows for x in range(WIDTH)]
    own = jnp.stack([own[h] for h in order])
    total, mine = learn(own, keys, values, lr_codes, depth)
    new = renew(total, mine, depth)
    return apply_fast(queries, new)


def column_squares(matrix):
    return jnp.sum(matrix * matrix, axis=1)


def rescale(moved, col_weight, col_moved):
    return moved * jnp.sqrt((col_weight + EPSILON) / (col_moved + EPSILON))[:, None, :]


def step_scale(col_weight, grad_total):
    return (
        STEP_SIZE * jnp.sqrt(jnp.sum(col_weight, axis=1) + EPSILON) / jnp.sqrt(grad_total + EPSILON)
    )


def apply_rows(queries, gate_b, up_b, down_b):
    query_gate = jnp.einsum("htd,hdf->htf", queries, gate_b, preferred_element_type=jnp.float32)
    query_up = jnp.einsum("htd,hdf->htf", queries, up_b, preferred_element_type=jnp.float32)
    query_hidden = (jax.nn.silu(query_gate) * query_up).astype(jnp.bfloat16)
    return jnp.einsum(
        "htf,hfd->htd", query_hidden, down_b, preferred_element_type=jnp.float32
    ).astype(jnp.bfloat16)


def local_grads_rows(keys, target, gate_b, up_b, down_b):
    gate_pre = jnp.einsum("htd,hdf->htf", keys, gate_b, preferred_element_type=jnp.float32)
    up_pre = jnp.einsum("htd,hdf->htf", keys, up_b, preferred_element_type=jnp.float32)
    sigmoid_gate = jax.nn.sigmoid(gate_pre)
    hidden = (gate_pre * sigmoid_gate * up_pre).astype(jnp.bfloat16)
    back = jnp.einsum("htd,hfd->htf", target, down_b, preferred_element_type=jnp.float32)
    grad_gate_pre = (back * up_pre * sigmoid_gate * (1.0 + gate_pre * (1.0 - sigmoid_gate))).astype(
        jnp.bfloat16
    )
    grad_up_pre = (back * gate_pre * sigmoid_gate).astype(jnp.bfloat16)
    grad_gate = jnp.einsum("htd,htf->hdf", keys, grad_gate_pre, preferred_element_type=jnp.float32)
    grad_up = jnp.einsum("htd,htf->hdf", keys, grad_up_pre, preferred_element_type=jnp.float32)
    grad_down = jnp.einsum("htf,htd->hfd", hidden, target, preferred_element_type=jnp.float32)
    return (grad_gate, grad_up, grad_down)


def on_device_rows(queries, keys, values, lr_codes, fast_gate, fast_up, fast_down):
    token_rates = (lr_codes.astype(jnp.float32) + 1.0) / 16.0
    target = (-token_rates[:, :, None] * values.astype(jnp.float32)).astype(jnp.bfloat16)
    gate_b, up_b, down_b = (
        lax.all_gather(fast_gate.astype(jnp.bfloat16), ("seq", "sub"), axis=1, tiled=True),
        lax.all_gather(fast_up.astype(jnp.bfloat16), ("seq", "sub"), axis=1, tiled=True),
        lax.all_gather(fast_down.astype(jnp.bfloat16), ("seq", "sub"), axis=1, tiled=True),
    )
    grad_gate, grad_up, grad_down = local_grads_rows(keys, target, gate_b, up_b, down_b)
    owned = (
        lax.psum_scatter(grad_gate, ("seq", "sub"), scatter_dimension=1, tiled=True),
        lax.psum_scatter(grad_up, ("seq", "sub"), scatter_dimension=1, tiled=True),
        lax.psum_scatter(grad_down, ("seq", "sub"), scatter_dimension=1, tiled=True),
    )
    weights = (fast_gate, fast_up, fast_down)
    grad_local = jnp.stack(
        [
            jnp.sum(owned[0] * owned[0], axis=(1, 2)),
            jnp.sum(owned[1] * owned[1], axis=(1, 2)),
            jnp.sum(owned[2] * owned[2], axis=(1, 2)),
        ],
        axis=1,
    )
    col_gate, col_up, col_down, grad_totals = lax.psum(
        (column_squares(fast_gate), column_squares(fast_up), column_squares(fast_down), grad_local),
        ("seq", "sub"),
    )
    col_weights = (col_gate, col_up, col_down)
    moved_all = []
    for index in range(3):
        scale = step_scale(col_weights[index], grad_totals[:, index])
        moved_all.append(weights[index] - scale[:, None, None] * owned[index])
    moved_cols = lax.psum(
        (column_squares(moved_all[0]), column_squares(moved_all[1]), column_squares(moved_all[2])),
        ("seq", "sub"),
    )
    renewed = [
        rescale(moved_all[index], col_weights[index], moved_cols[index]).astype(jnp.bfloat16)
        for index in range(3)
    ]
    new_gate, new_up, new_down = (
        lax.all_gather(renewed[0], ("seq", "sub"), axis=1, tiled=True),
        lax.all_gather(renewed[1], ("seq", "sub"), axis=1, tiled=True),
        lax.all_gather(renewed[2], ("seq", "sub"), axis=1, tiled=True),
    )
    return apply_rows(queries, new_gate, new_up, new_down)


def solution(mesh):
    groups, seq, sub = (mesh.shape[axis] for axis in ("groups", "seq", "sub"))

    def on_device(*arrays):
        if groups == 2 and sub == 2 and seq % (2 * WIDTH) == 0 and arrays[4].shape[0] == seq:
            return on_device_heads(seq // WIDTH, *arrays)
        return on_device_rows(*arrays)

    return jax.shard_map(
        on_device,
        mesh=mesh,
        in_specs=(
            P("head", ("groups", "seq", "sub"), None),
            P("head", ("groups", "seq", "sub"), None),
            P("head", ("groups", "seq", "sub"), None),
            P("head", ("groups", "seq", "sub")),
            P("head", ("seq", "sub"), None),
            P("head", ("seq", "sub"), None),
            P("head", ("seq", "sub"), None),
        ),
        out_specs=P("head", ("groups", "seq", "sub"), None),
        check_vma=False,
    )
```
